32 devices in a mesh: seqhi: 4 (over x, core), seqlo: 8 (over z, y).
Axes of the slice: x: 2, y: 2, z: 4, core: 2. Of those that a mesh axis runs over, the one named last changes fastest.
Arguments:
- features: float32 [8192, 256], P(('seqhi', 'seqlo')), may hold values from -6 to 6
- norm_gain: float32 [8, 512], replicated, may hold values from 0.1 to 1.9
- bias_hidden: float32 [8, 1024], replicated, may hold values from -4 to 4
- gate_logit: float32 [8, 512], replicated, may hold values from -2 to 2
- w_in: float32 [512, 1024], replicated, may hold values from -0.25 to 0.25
- w_out: float32 [1024, 512], replicated, may hold values from -0.1875 to 0.1875
Outputs:
- switched: float32 [8192, 256], P(('seqhi', 'seqlo'))
The draws below stay inside these ranges and needn't reach their ends.
All inputs are finite; a program needn't handle non-finite values.
Results may differ from the reference program's by a relative error of at most 0.0001.
Values sent between devices are 32-bit elements; how exact they have to be, the bound alone decides.
No kernel may reach another device: no remote copies, remote signals or barrier semaphores. Data moves between devices by JAX's collectives and lax.ppermute only.
A program may use at most 64 MiB of HBM per device.

```python
import jax
import jax.numpy as jnp
from jax import lax

W = 256
HID = 1024
HI_LAYERS = 4
LO_LAYERS = 4
POS_DEV = 256
LAYERS = 8
NPOS = 8192
N_SEQHI = 4
N_SEQLO = 8


def levels(rng, extent, pieces, least, top_value):
    level = 1.0
    for position, parts in pieces:
        steps = jax.random.uniform(jax.random.fold_in(jax.random.fold_in(rng, 6), position), (parts,), jnp.float32, least / len(pieces), top_value / len(pieces))
        level = level * jnp.repeat(jnp.exp(steps), extent[position] // parts).reshape((-1,) + (1,) * (len(extent) - 1 - position))
    return level


def gaussian(own_key, extent, width, bound, split=(), dtype=jnp.bfloat16):
    factor_of = levels(own_key, extent, split, -0.22, 0.18) if split else 1.0
    entries = jax.random.normal(own_key, extent, jnp.float32) * width * factor_of
    return jnp.minimum(jnp.maximum(entries, -bound), bound).astype(dtype)


def setup_inputs(seed: int = 0) -> dict:
    streams_of = jax.random.split(jax.random.key(seed), 7)
    return {
        "features": gaussian(streams_of[0], (NPOS, W), 1.0, 6.0, ((0, 32),), jnp.float32),
        "norm_gain": jnp.clip(1.0 + 0.18 * jax.random.normal(streams_of[1], (LAYERS, 2 * W), jnp.float32), 0.1, 1.9),
        "bias_hidden": gaussian(streams_of[2], (LAYERS, HID), 1.0, 4.0, (), jnp.float32),
        "gate_logit": jnp.clip(jax.random.uniform(streams_of[3], (LAYERS, 2 * W), jnp.float32, -2.0, 2.0), -2.0, 2.0),
        "w_in": gaussian(streams_of[4], (2 * W, HID), (2 * W) ** -0.5, 0.25, (), jnp.float32),
        "w_out": gaussian(streams_of[5], (HID, 2 * W), HID ** -0.5, 0.1875, (), jnp.float32),
    }


NORM_EPS = 1e-05

def switch_unit(lower_rows, upper_rows, layer_params):
    norm_gain, bias_hidden, gate_logit, w_in, w_out = layer_params
    feature_count = lower_rows.shape[-1]
    paired = jnp.concatenate([lower_rows, upper_rows], axis=-1)
    center = paired - lax.optimization_barrier(jnp.mean(paired, axis=-1, keepdims=True))
    spread = lax.optimization_barrier(jnp.mean(center * center, axis=-1, keepdims=True))
    normed = center * lax.rsqrt(spread + NORM_EPS) * norm_gain
    hidden = jax.nn.gelu(jnp.dot(normed, w_in, precision=lax.Precision.HIGHEST, preferred_element_type=jnp.float32) + bias_hidden)
    mixed_out = jax.nn.sigmoid(gate_logit) * paired + jnp.dot(hidden, w_out, precision=lax.Precision.HIGHEST, preferred_element_type=jnp.float32)
    return (mixed_out[:, :feature_count], mixed_out[:, feature_count:])

def pair_layer(states, distance, layer_params):
    row_count, feature_count = states.shape
    groups = row_count // (2 * distance)
    grouped = states.reshape(groups, 2, distance, feature_count)
    new_lower, new_upper = switch_unit(grouped[:, 0].reshape(-1, feature_count), grouped[:, 1].reshape(-1, feature_count), layer_params)
    joined = jnp.stack([new_lower.reshape(groups, distance, feature_count), new_upper.reshape(groups, distance, feature_count)], axis=1)
    return joined.reshape(row_count, feature_count)

def reference(features, norm_gain, bias_hidden, gate_logit, w_in, w_out):
    high_bits = N_SEQHI.bit_length() - 1
    low_bits = N_SEQLO.bit_length() - 1
    states = features
    for layer_index in range(HI_LAYERS + LO_LAYERS):
        if layer_index < HI_LAYERS:
            distance = POS_DEV * N_SEQLO * 2 ** (layer_index % high_bits)
        else:
            distance = POS_DEV * 2 ** ((layer_index - HI_LAYERS) % low_bits)
        layer_params = (norm_gain[layer_index], bias_hidden[layer_index], gate_logit[layer_index], w_in, w_out)
        states = pair_layer(states, distance, layer_params)
    return states
```

```python
import functools

import jax
import jax.numpy as jnp
from jax import lax
from jax.experimental import pallas as pl
from jax.experimental.pallas import tpu as pltpu
from jax.sharding import PartitionSpec as P

HI_LAYERS = 4
NORM_EPS = 1e-05
GELU_SCALE = 0.7978845608028654
GELU_CUBE = 0.044715


def split_high_low(x):
    high = x.astype(jnp.bfloat16)
    return high, (x - high.astype(jnp.float32)).astype(jnp.bfloat16)


def dot(a, b):
    return jnp.dot(a, b, preferred_element_type=jnp.float32)


def dot_split(x, w_high, w_low):
    rows = x.shape[0]
    x_high, x_low = split_high_low(x)
    both = dot(jnp.concatenate([x_high, x_low], axis=0), w_high)
    return both[:rows] + (both[rows:] + dot(x_high, w_low))


def gelu(x):
    return 0.5 * x * (1.0 + jnp.tanh(GELU_SCALE * (x + GELU_CUBE * (x * x * x))))


def switch_unit(lower, upper, gain, bias, gate, w_in, w_out, hidden_block):
    width = lower.shape[-1]
    pair = jnp.concatenate([lower, upper], axis=-1)
    center = pair - jnp.mean(pair, axis=-1, keepdims=True)
    spread = jnp.mean(center * center, axis=-1, keepdims=True)
    normed = center * lax.rsqrt(spread + NORM_EPS) * gain
    out = gate * pair
    in_high, in_low = w_in
    out_high, out_low = w_out
    for start in range(0, in_high.shape[1], hidden_block):
        cols = slice(start, start + hidden_block)
        hidden = gelu(dot_split(normed, in_high[:, cols], in_low[:, cols]) + bias[:, cols])
        out = out + dot_split(hidden, out_high[cols, :], out_low[cols, :])
    return out[:, :width], out[:, width:]


def layers_kernel(
    first, distances, hidden_block,
    x_ref, gain_ref, bias_ref, gate_ref, in_high_ref, in_low_ref, out_high_ref, out_low_ref, y_ref,
):
    rows, width = x_ref.shape
    states = x_ref[...]
    for step, distance in enumerate(distances):
        k = first + step
        groups = rows // (2 * distance)
        grouped = states.reshape(groups, 2, distance, width)
        new_lower, new_upper = switch_unit(
            grouped[:, 0].reshape(-1, width),
            grouped[:, 1].reshape(-1, width),
            gain_ref[k : k + 1, :],
            bias_ref[k : k + 1, :],
            jax.nn.sigmoid(gate_ref[k : k + 1, :]),
            (in_high_ref, in_low_ref),
            (out_high_ref, out_low_ref),
            hidden_block,
        )
        shape = (groups, 1, distance, width)
        states = jnp.concatenate(
            [new_lower.reshape(shape), new_upper.reshape(shape)], axis=1
        ).reshape(rows, width)
    y_ref[...] = states.reshape(y_ref.shape)


def run_layers(states, first, distances, params, name):
    rows, width = states.shape
    hidden = params[1].shape[1]
    kernel = functools.partial(layers_kernel, first, distances, min(hidden, 256))
    return pl.pallas_call(
        kernel,
        out_shape=jax.ShapeDtypeStruct((rows, width), jnp.float32),
        in_specs=[pl.BlockSpec(memory_space=pltpu.VMEM)] * 8,
        out_specs=pl.BlockSpec(memory_space=pltpu.VMEM),
        compiler_params=pltpu.CompilerParams(vmem_limit_bytes=24 * 2**20),
        name=name,
    )(states, *params)


def swap_leading(x, a, b):
    return x.reshape(a, b, -1, x.shape[-1]).swapaxes(0, 1).reshape(x.shape)


def all_to_all(x, axes):
    return lax.all_to_all(x, axes, split_axis=0, concat_axis=0, tiled=True)


def body(features, norm_gain, bias_hidden, gate_logit, w_in, w_out):
    rows = features.shape[0]
    high_count = lax.axis_size("seqhi")
    low_count = lax.axis_size("seqlo")
    high_bits = high_count.bit_length() - 1
    low_bits = low_count.bit_length() - 1
    layer_total = norm_gain.shape[0]

    def parts(w):
        high = lax.reduce_precision(w, exponent_bits=8, mantissa_bits=7)
        return high.astype(jnp.bfloat16), (w - high).astype(jnp.bfloat16)

    params = (norm_gain, bias_hidden, gate_logit, *parts(w_in), *parts(w_out))
    high_distances = [rows // high_count * 2 ** (k % high_bits) for k in range(HI_LAYERS)]
    low_distances = [rows // low_count * 2 ** (j % low_bits) for j in range(layer_total - HI_LAYERS)]

    states = all_to_all(features, "seqhi")
    states = run_layers(states, 0, high_distances, params, "high_layers")
    if rows % (8 * high_count * low_count) == 0:
        states = swap_leading(states, high_count, low_count)
        states = all_to_all(states, "seqlo")
        states = run_layers(states, HI_LAYERS, low_distances, params, "low_layers")
        states = swap_leading(states, low_count, high_count)
        return all_to_all(states, ("seqhi", "seqlo"))
    states = all_to_all(states, "seqhi")
    states = all_to_all(states, "seqlo")
    states = run_layers(states, HI_LAYERS, low_distances, params, "low_layers")
    return all_to_all(states, "seqlo")


def solution(mesh):
    placed = (P(("seqhi", "seqlo"), None), P(), P(), P(), P(), P())
    return jax.shard_map(
        body, mesh=mesh, in_specs=placed, out_specs=P(("seqhi", "seqlo"), None), check_vma=False
    )
```

```python
import functools

import jax
import jax.numpy as jnp
from jax import lax
from jax.experimental import pallas as pl
from jax.experimental.pallas import tpu as pltpu
from jax.sharding import PartitionSpec as P

HI_LAYERS = 4
NORM_EPS = 1e-05
GELU_SCALE = 0.7978845608028654
GELU_CUBE = 0.044715
AXES = ("seqhi", "seqlo")
VMEM = pl.BlockSpec(memory_space=pltpu.VMEM)


def split_high_low(x):
    high = x.astype(jnp.bfloat16)
    return high, (x - high.astype(jnp.float32)).astype(jnp.bfloat16)


def dot(a, b):
    return jnp.dot(a, b, preferred_element_type=jnp.float32)


def dot_split(x, w_high, w_low):
    rows = x.shape[0]
    x_high, x_low = split_high_low(x)
    both = dot(jnp.concatenate([x_high, x_low], axis=0), w_high)
    return both[:rows] + (both[rows:] + dot(x_high, w_low))


def gelu(x):
    return 0.5 * x * (1.0 + jnp.tanh(GELU_SCALE * (x + GELU_CUBE * (x * x * x))))


def switch_unit(lower, upper, gain, bias, gate, w_in, w_out, hidden_block):
    width = lower.shape[-1]
    pair = jnp.concatenate([lower, upper], axis=-1)
    center = pair - jnp.mean(pair, axis=-1, keepdims=True)
    spread = jnp.mean(center * center, axis=-1, keepdims=True)
    normed = center * lax.rsqrt(spread + NORM_EPS) * gain
    out = gate * pair
    in_high, in_low = w_in
    out_high, out_low = w_out
    for start in range(0, in_high.shape[1], hidden_block):
        cols = slice(start, start + hidden_block)
        hidden = gelu(dot_split(normed, in_high[:, cols], in_low[:, cols]) + bias[:, cols])
        out = out + dot_split(hidden, out_high[cols, :], out_low[cols, :])
    return out[:, :width], out[:, width:]


def layers_kernel(first, distances, hidden_block, axis, chunks_out, send_from, *refs):
    chunks_in = lax.axis_size(axis)
    x_refs = refs[:chunks_in]
    gain_ref, bias_ref, gate_ref, in_high_ref, in_low_ref, out_high_ref, out_low_ref = refs[
        chunks_in : chunks_in + 7
    ]
    y_refs = refs[chunks_in + 7 : -2]
    arrived, leaving = refs[-2:]
    me = lax.axis_index(axis)
    for step, x_ref in enumerate(x_refs):
        arrived[me ^ step] = x_ref[...]
    count, chunk, width = arrived.shape
    rows = count * chunk
    states = arrived[...].reshape(rows, width)
    for step, distance in enumerate(distances):
        k = first + step
        groups = rows // (2 * distance)
        grouped = states.reshape(groups, 2, distance, width)
        new_lower, new_upper = switch_unit(
            grouped[:, 0].reshape(-1, width),
            grouped[:, 1].reshape(-1, width),
            gain_ref[k : k + 1, :],
            bias_ref[k : k + 1, :],
            jax.nn.sigmoid(gate_ref[k : k + 1, :]),
            (in_high_ref, in_low_ref),
            (out_high_ref, out_low_ref),
            hidden_block,
        )
        shape = (groups, 1, distance, width)
        states = jnp.concatenate(
            [new_lower.reshape(shape), new_upper.reshape(shape)], axis=1
        ).reshape(rows, width)
    leaving[...] = states.reshape(leaving.shape)
    first_chunk = send_from()
    for step, y_ref in enumerate(y_refs):
        y_ref[...] = leaving[first_chunk ^ step]


def run_layers(chunks, first, distances, axis, chunks_out, send_from, params, name):
    chunk, width = chunks[0].shape
    rows = chunk * len(chunks)
    hidden = params[1].shape[1]
    kernel = functools.partial(
        layers_kernel, first, distances, min(hidden, 256), axis, chunks_out, send_from
    )
    return pl.pallas_call(
        kernel,
        out_shape=[jax.ShapeDtypeStruct((rows // chunks_out, width), jnp.float32)] * chunks_out,
        in_specs=[VMEM] * (len(chunks) + 7),
        out_specs=[VMEM] * chunks_out,
        scratch_shapes=[
            pltpu.VMEM((len(chunks), chunk, width), jnp.float32),
            pltpu.VMEM((chunks_out, rows // chunks_out, width), jnp.float32),
        ],
        compiler_params=pltpu.CompilerParams(vmem_limit_bytes=24 * 2**20),
        name=name,
    )(*chunks, *params)


def take_apart_kernel(axis, x_ref, *y_refs):
    me = lax.axis_index(axis)
    for step, y_ref in enumerate(y_refs):
        y_ref[...] = x_ref[me ^ step]


def take_apart(x, axis, count):
    rows, width = x.shape
    return pl.pallas_call(
        functools.partial(take_apart_kernel, axis),
        out_shape=[jax.ShapeDtypeStruct((rows // count, width), jnp.float32)] * count,
        in_specs=[VMEM],
        out_specs=[VMEM] * count,
        name="take_apart",
    )(x.reshape(count, rows // count, width))


def put_together_kernel(axis, *refs):
    me = lax.axis_index(axis)
    y_ref = refs[-1]
    for step, x_ref in enumerate(refs[:-1]):
        y_ref[me ^ step] = x_ref[...]


def put_together(chunks, axis):
    chunk, width = chunks[0].shape
    return pl.pallas_call(
        functools.partial(put_together_kernel, axis),
        out_shape=jax.ShapeDtypeStruct((len(chunks), chunk, width), jnp.float32),
        in_specs=[VMEM] * len(chunks),
        out_specs=VMEM,
        name="put_together",
    )(*chunks).reshape(-1, width)


def exchange(chunks, axis):
    count = len(chunks)
    return [chunks[0]] + [
        lax.ppermute(chunks[step], axis, [(i, i ^ step) for i in range(count)])
        for step in range(1, count)
    ]


def body(features, norm_gain, bias_hidden, gate_logit, w_in, w_out):
    rows = features.shape[0]
    high_count = lax.axis_size("seqhi")
    low_count = lax.axis_size("seqlo")
    high_bits = high_count.bit_length() - 1
    low_bits = low_count.bit_length() - 1
    layer_total = norm_gain.shape[0]
    spare = low_count // high_count

    def parts(w):
        high = lax.reduce_precision(w, exponent_bits=8, mantissa_bits=7)
        return high.astype(jnp.bfloat16), (w - high).astype(jnp.bfloat16)

    params = (norm_gain, bias_hidden, gate_logit, *parts(w_in), *parts(w_out))
    high_distances = [rows // high_count * 2 ** (k % high_bits) for k in range(HI_LAYERS)]
    low_distances = [rows // low_count * 2 ** (j % low_bits) for j in range(layer_total - HI_LAYERS)]

    def low_index():
        return lax.axis_index("seqlo")

    def row_index():
        return lax.axis_index("seqhi") * spare + lax.rem(lax.axis_index("seqlo"), spare)

    chunks = exchange(take_apart(features, "seqhi", high_count), "seqhi")
    chunks = run_layers(
        chunks, 0, high_distances, "seqhi", low_count, low_index, params, "high_layers"
    )
    chunks = exchange(chunks, "seqlo")
    chunks = run_layers(
        chunks, HI_LAYERS, low_distances, "seqlo", low_count, row_index, params, "low_layers"
    )
    home = []
    for step in range(low_count):
        pairs = []
        for high in range(high_count):
            for low in range(low_count):
                block = high * spare + low % spare
                target = (low // spare) * low_count + (block ^ step)
                pairs.append((high * low_count + low, target))
        home.append(lax.ppermute(chunks[step], AXES, pairs))
    return put_together(home, "seqlo")


def solution(mesh):
    placed = (P(AXES, None), P(), P(), P(), P(), P())
    return jax.shard_map(
        body, mesh=mesh, in_specs=placed, out_specs=P(AXES, None), check_vma=False
    )
```

```python
import functools

import jax
import jax.numpy as jnp
from jax import lax
from jax.experimental import pallas as pl
from jax.experimental.pallas import tpu as pltpu
from jax.sharding import PartitionSpec as P

HI_LAYERS = 4
NORM_EPS = 1e-05
GELU_SCALE = 0.7978845608028654
GELU_CUBE = 0.044715


def split_high_low(x):
    high = x.astype(jnp.bfloat16)
    return high, (x - high.astype(jnp.float32)).astype(jnp.bfloat16)


def dot(a, b):
    return jnp.dot(a, b, preferred_element_type=jnp.float32)


def dot_split(x, w_high, w_low):
    rows = x.shape[0]
    x_high, x_low = split_high_low(x)
    both = dot(jnp.concatenate([x_high, x_low], axis=0), w_high)
    return both[:rows] + (both[rows:] + dot(x_high, w_low))


def gelu(x):
    return 0.5 * x * (1.0 + jnp.tanh(GELU_SCALE * (x + GELU_CUBE * (x * x * x))))


def switch_unit(lower, upper, gain, bias, gate, w_in, w_out, hidden_block):
    width = lower.shape[-1]
    pair = jnp.concatenate([lower, upper], axis=-1)
    center = pair - jnp.mean(pair, axis=-1, keepdims=True)
    spread = jnp.mean(center * center, axis=-1, keepdims=True)
    normed = center * lax.rsqrt(spread + NORM_EPS) * gain
    out = gate * pair
    in_high, in_low = w_in
    out_high, out_low = w_out
    for start in range(0, in_high.shape[1], hidden_block):
        cols = slice(start, start + hidden_block)
        hidden = gelu(dot_split(normed, in_high[:, cols], in_low[:, cols]) + bias[:, cols])
        out = out + dot_split(hidden, out_high[cols, :], out_low[cols, :])
    return out[:, :width], out[:, width:]


def layers_kernel(
    first, distances, hidden_block,
    x_ref, gain_ref, bias_ref, gate_ref, in_high_ref, in_low_ref, out_high_ref, out_low_ref, y_ref,
):
    rows, width = x_ref.shape
    states = x_ref[...]
    for step, distance in enumerate(distances):
        k = first + step
        groups = rows // (2 * distance)
        grouped = states.reshape(groups, 2, distance, width)
        new_lower, new_upper = switch_unit(
            grouped[:, 0].reshape(-1, width),
            grouped[:, 1].reshape(-1, width),
            gain_ref[k : k + 1, :],
            bias_ref[k : k + 1, :],
            jax.nn.sigmoid(gate_ref[k : k + 1, :]),
            (in_high_ref, in_low_ref),
            (out_high_ref, out_low_ref),
            hidden_block,
        )
        shape = (groups, 1, distance, width)
        states = jnp.concatenate(
            [new_lower.reshape(shape), new_upper.reshape(shape)], axis=1
        ).reshape(rows, width)
    y_ref[...] = states


def run_layers(states, first, distances, params, name):
    rows, width = states.shape
    hidden = params[1].shape[1]
    kernel = functools.partial(layers_kernel, first, distances, min(hidden, 256))
    return pl.pallas_call(
        kernel,
        out_shape=jax.ShapeDtypeStruct((rows, width), jnp.float32),
        in_specs=[pl.BlockSpec(memory_space=pltpu.VMEM)] * 8,
        out_specs=pl.BlockSpec(memory_space=pltpu.VMEM),
        compiler_params=pltpu.CompilerParams(vmem_limit_bytes=24 * 2**20),
        name=name,
    )(states, *params)


def all_to_all(x, axes):
    return lax.all_to_all(x, axes, split_axis=0, concat_axis=0, tiled=True)


def body(features, norm_gain, bias_hidden, gate_logit, w_in, w_out):
    rows = features.shape[0]
    high_count = lax.axis_size("seqhi")
    low_count = lax.axis_size("seqlo")
    high_bits = high_count.bit_length() - 1
    low_bits = low_count.bit_length() - 1
    layer_total = norm_gain.shape[0]

    def parts(w):
        high = lax.reduce_precision(w, exponent_bits=8, mantissa_bits=7)
        return high.astype(jnp.bfloat16), (w - high).astype(jnp.bfloat16)

    params = (norm_gain, bias_hidden, gate_logit, *parts(w_in), *parts(w_out))
    if rows % (8 * high_count * low_count) == 0:
        states = all_to_all(features, ("seqhi", "seqlo"))
        distances = [rows // high_count * 2 ** (k % high_bits) for k in range(HI_LAYERS)]
        distances += [
            rows // (high_count * low_count) * 2 ** (j % low_bits)
            for j in range(layer_total - HI_LAYERS)
        ]
        states = run_layers(states, 0, distances, params, "all_layers")
        return all_to_all(states, ("seqhi", "seqlo"))
    high_distances = [rows // high_count * 2 ** (k % high_bits) for k in range(HI_LAYERS)]
    low_distances = [rows // low_count * 2 ** (j % low_bits) for j in range(layer_total - HI_LAYERS)]
    states = all_to_all(features, "seqhi")
    states = run_layers(states, 0, high_distances, params, "high_layers")
    states = all_to_all(states, "seqhi")
    states = all_to_all(states, "seqlo")
    states = run_layers(states, HI_LAYERS, low_distances, params, "low_layers")
    return all_to_all(states, "seqlo")


def solution(mesh):
    placed = (P(("seqhi", "seqlo"), None), P(), P(), P(), P(), P())
    return jax.shard_map(
        body, mesh=mesh, in_specs=placed, out_specs=P(("seqhi", "seqlo"), None), check_vma=False
    )
```

```python
import functools

import jax
import jax.numpy as jnp
from jax import lax
from jax.experimental import pallas as pl
from jax.experimental.pallas import tpu as pltpu
from jax.sharding import PartitionSpec as P

HI_LAYERS = 4
NORM_EPS = 1e-05
GELU_SCALE = 0.7978845608028654
GELU_CUBE = 0.044715


def split_high_low(x):
    high = x.astype(jnp.bfloat16)
    return high, (x - high.astype(jnp.float32)).astype(jnp.bfloat16)


def dot_split(x, w_high, w_low):
    x_high, x_low = split_high_low(x)
    return jnp.dot(
        jnp.concatenate([x_high, x_high, x_low], axis=1),
        jnp.concatenate([w_high, w_low, w_high], axis=0),
        preferred_element_type=jnp.float32,
    )


def gelu(x):
    return 0.5 * x * (1.0 + jnp.tanh(GELU_SCALE * (x + GELU_CUBE * (x * x * x))))


def switch_unit(lower, upper, gain, bias, gate, w_in, w_out, hidden_block):
    width = lower.shape[-1]
    pair = jnp.concatenate([lower, upper], axis=-1)
    center = pair - jnp.mean(pair, axis=-1, keepdims=True)
    spread = jnp.mean(center * center, axis=-1, keepdims=True)
    normed = center * lax.rsqrt(spread + NORM_EPS) * gain
    out = gate * pair
    in_high, in_low = w_in
    out_high, out_low = w_out
    for start in range(0, in_high.shape[1], hidden_block):
        cols = slice(start, start + hidden_block)
        hidden = gelu(dot_split(normed, in_high[:, cols], in_low[:, cols]) + bias[:, cols])
        out = out + dot_split(hidden, out_high[cols, :], out_low[cols, :])
    return out[:, :width], out[:, width:]


def layers_kernel(
    first, distances, hidden_block,
    x_ref, gain_ref, bias_ref, gate_ref, in_high_ref, in_low_ref, out_high_ref, out_low_ref, y_ref,
):
    rows, width = x_ref.shape
    states = x_ref[...]
    for step, distance in enumerate(distances):
        k = first + step
        groups = rows // (2 * distance)
        grouped = states.reshape(groups, 2, distance, width)
        new_lower, new_upper = switch_unit(
            grouped[:, 0].reshape(-1, width),
            grouped[:, 1].reshape(-1, width),
            gain_ref[k : k + 1, :],
            bias_ref[k : k + 1, :],
            jax.nn.sigmoid(gate_ref[k : k + 1, :]),
            (in_high_ref, in_low_ref),
            (out_high_ref, out_low_ref),
            hidden_block,
        )
        shape = (groups, 1, distance, width)
        states = jnp.concatenate(
            [new_lower.reshape(shape), new_upper.reshape(shape)], axis=1
        ).reshape(rows, width)
    y_ref[...] = states


def run_layers(states, first, distances, params, name):
    rows, width = states.shape
    hidden = params[1].shape[1]
    kernel = functools.partial(layers_kernel, first, distances, min(hidden, 256))
    return pl.pallas_call(
        kernel,
        out_shape=jax.ShapeDtypeStruct((rows, width), jnp.float32),
        in_specs=[pl.BlockSpec(memory_space=pltpu.VMEM)] * 8,
        out_specs=pl.BlockSpec(memory_space=pltpu.VMEM),
        compiler_params=pltpu.CompilerParams(vmem_limit_bytes=12 * 2**20),
        name=name,
    )(states, *params)


def all_to_all(x, axes):
    return lax.all_to_all(x, axes, split_axis=0, concat_axis=0, tiled=True)


def body(features, norm_gain, bias_hidden, gate_logit, w_in, w_out):
    rows = features.shape[0]
    high_count = lax.axis_size("seqhi")
    low_count = lax.axis_size("seqlo")
    high_bits = high_count.bit_length() - 1
    low_bits = low_count.bit_length() - 1
    layer_total = norm_gain.shape[0]

    def parts(w):
        high = lax.reduce_precision(w, exponent_bits=8, mantissa_bits=7)
        return high.astype(jnp.bfloat16), (w - high).astype(jnp.bfloat16)

    params = (norm_gain, bias_hidden, gate_logit, *parts(w_in), *parts(w_out))
    if rows % (8 * high_count * low_count) == 0:
        states = all_to_all(features, ("seqhi", "seqlo"))
        distances = [rows // high_count * 2 ** (k % high_bits) for k in range(HI_LAYERS)]
        distances += [
            rows // (high_count * low_count) * 2 ** (j % low_bits)
            for j in range(layer_total - HI_LAYERS)
        ]
        states = run_layers(states, 0, distances, params, "all_layers")
        return all_to_all(states, ("seqhi", "seqlo"))
    high_distances = [rows // high_count * 2 ** (k % high_bits) for k in range(HI_LAYERS)]
    low_distances = [rows // low_count * 2 ** (j % low_bits) for j in range(layer_total - HI_LAYERS)]
    states = all_to_all(features, "seqhi")
    states = run_layers(states, 0, high_distances, params, "high_layers")
    states = all_to_all(states, "seqhi")
    states = all_to_all(states, "seqlo")
    states = run_layers(states, HI_LAYERS, low_distances, params, "low_layers")
    return all_to_all(states, "seqlo")


def solution(mesh):
    placed = (P(("seqhi", "seqlo"), None), P(), P(), P(), P(), P())
    return jax.shard_map(
        body, mesh=mesh, in_specs=placed, out_specs=P(("seqhi", "seqlo"), None), check_vma=False
    )
```

```python
import functools

import jax
import jax.numpy as jnp
from jax import lax
from jax.experimental import pallas as pl
from jax.experimental.pallas import tpu as pltpu
from jax.sharding import PartitionSpec as P

HI_LAYERS = 4
NORM_EPS = 1e-05
GELU_SCALE = 0.7978845608028654
GELU_CUBE = 0.044715


def split_high_low(x):
    high = x.astype(jnp.bfloat16)
    return high, (x - high.astype(jnp.float32)).astype(jnp.bfloat16)


def dot(a, b):
    return jnp.dot(a, b, preferred_element_type=jnp.float32)


def dot_split(x, w_high, w_low):
    rows = x.shape[0]
    x_high, x_low = split_high_low(x)
    both = dot(jnp.concatenate([x_high, x_low], axis=0), w_high)
    return both[:rows] + (both[rows:] + dot(x_high, w_low))


def gelu(x):
    return 0.5 * x * (1.0 + jnp.tanh(GELU_SCALE * (x + GELU_CUBE * (x * x * x))))


def split_rows(distances, rows):
    strides = [8 * 2**i for i in range((rows // 16).bit_length())]
    runs, start = [], 0
    while start < len(distances):
        end, stride = start, None
        while end < len(distances):
            free = [s for s in strides if s not in distances[start : end + 1]]
            if not free:
                break
            end, stride = end + 1, free[-1]
        end = max(end, start + 1)
        runs.append((start, end, stride))
        start = end
    return runs


def layer_chain(states, layers, hidden_block, weights):
    rows, width = states.shape
    gain_ref, bias_ref, gate_ref, in_high, in_low, out_high, out_low, ready = weights
    hidden_count = in_high.shape[1]
    for k, distance in layers:
        groups = rows // (2 * distance)
        grouped = states.reshape(groups, 2, distance, width)
        pair = jnp.concatenate(
            [grouped[:, 0].reshape(-1, width), grouped[:, 1].reshape(-1, width)], axis=-1
        )
        center = pair - jnp.mean(pair, axis=-1, keepdims=True)
        spread = jnp.mean(center * center, axis=-1, keepdims=True)
        normed = center * lax.rsqrt(spread + NORM_EPS) * gain_ref[k : k + 1, :]
        out = jax.nn.sigmoid(gate_ref[k : k + 1, :]) * pair
        yield None
        blocks = [slice(c, c + hidden_block) for c in range(0, hidden_count, hidden_block)]
        for cols in blocks:
            mixed = dot_split(normed, in_high[:, cols], in_low[:, cols])
            hidden = gelu(mixed + bias_ref[k : k + 1, cols])
            yield None
            ready()
            out = out + dot_split(hidden, out_high[cols, :], out_low[cols, :])
            yield None
        shape = (groups, 1, distance, width)
        states = jnp.concatenate(
            [out[:, :width].reshape(shape), out[:, width:].reshape(shape)], axis=1
        ).reshape(rows, width)
    yield states


def interleave(chains, lag):
    results = [None] * len(chains)
    active = list(range(len(chains)))
    turn = 0
    while active:
        for i in list(active):
            if turn < i * lag:
                continue
            value = next(chains[i])
            if value is not None:
                results[i] = value
                active.remove(i)
        turn += 1
    return results


def layers_kernel(
    first, distances, hidden_block,
    x_ref, gain_ref, bias_ref, gate_ref, in_high_ref, in_low_ref, out_low_ref, out_high_hbm,
    y_ref, out_high_ref, copied,
):
    copy = pltpu.make_async_copy(out_high_hbm, out_high_ref, copied)
    copy.start()
    waited = []

    def ready():
        if not waited:
            copy.wait()
            waited.append(True)

    weights = (gain_ref, bias_ref, gate_ref, in_high_ref, in_low_ref, out_high_ref, out_low_ref, ready)
    rows, width = x_ref.shape
    states = x_ref[...]
    for start, end, stride in split_rows(distances, rows):
        ks = range(first + start, first + end)
        if stride is None:
            layers = list(zip(ks, distances[start:end]))
            (states,) = interleave([layer_chain(states, layers, hidden_block, weights)], 0)
            continue
        parted = states.reshape(rows // (2 * stride), 2, stride, width)
        layers = [(k, d if d < stride else d // 2) for k, d in zip(ks, distances[start:end])]
        halves = interleave(
            [
                layer_chain(parted[:, i].reshape(rows // 2, width), layers, hidden_block, weights)
                for i in range(2)
            ],
            2,
        )
        shape = (rows // (2 * stride), 1, stride, width)
        states = jnp.concatenate([half.reshape(shape) for half in halves], axis=1)
        states = states.reshape(rows, width)
    y_ref[...] = states


def run_layers(states, first, distances, params, name):
    rows, width = states.shape
    hidden = params[1].shape[1]
    kernel = functools.partial(layers_kernel, first, distances, min(hidden, 512))
    vmem = pl.BlockSpec(memory_space=pltpu.VMEM)
    return pl.pallas_call(
        kernel,
        out_shape=jax.ShapeDtypeStruct((rows, width), jnp.float32),
        in_specs=[vmem] * 7 + [pl.BlockSpec(memory_space=pltpu.HBM)],
        out_specs=vmem,
        scratch_shapes=[pltpu.VMEM(params[-1].shape, params[-1].dtype), pltpu.SemaphoreType.DMA],
        compiler_params=pltpu.CompilerParams(vmem_limit_bytes=16 * 2**20),
        name=name,
    )(states, *params)


def all_to_all(x, axes):
    return lax.all_to_all(x, axes, split_axis=0, concat_axis=0, tiled=True)


def body(features, norm_gain, bias_hidden, gate_logit, w_in, w_out):
    rows = features.shape[0]
    high_count = lax.axis_size("seqhi")
    low_count = lax.axis_size("seqlo")
    high_bits = high_count.bit_length() - 1
    low_bits = low_count.bit_length() - 1
    layer_total = norm_gain.shape[0]

    def parts(w):
        high = lax.reduce_precision(w, exponent_bits=8, mantissa_bits=7)
        return high.astype(jnp.bfloat16), (w - high).astype(jnp.bfloat16)

    out_high, out_low = parts(w_out)
    params = (norm_gain, bias_hidden, gate_logit, *parts(w_in), out_low, out_high)
    if rows % (8 * high_count * low_count) == 0:
        states = all_to_all(features, ("seqhi", "seqlo"))
        distances = [rows // high_count * 2 ** (k % high_bits) for k in range(HI_LAYERS)]
        distances += [
            rows // (high_count * low_count) * 2 ** (j % low_bits)
            for j in range(layer_total - HI_LAYERS)
        ]
        states = run_layers(states, 0, distances, params, "all_layers")
        return all_to_all(states, ("seqhi", "seqlo"))
    high_distances = [rows // high_count * 2 ** (k % high_bits) for k in range(HI_LAYERS)]
    low_distances = [rows // low_count * 2 ** (j % low_bits) for j in range(layer_total - HI_LAYERS)]
    states = all_to_all(features, "seqhi")
    states = run_layers(states, 0, high_distances, params, "high_layers")
    states = all_to_all(states, "seqhi")
    states = all_to_all(states, "seqlo")
    states = run_layers(states, HI_LAYERS, low_distances, params, "low_layers")
    return all_to_all(states, "seqlo")


def solution(mesh):
    placed = (P(("seqhi", "seqlo"), None), P(), P(), P(), P(), P())
    return jax.shard_map(
        body, mesh=mesh, in_specs=placed, out_specs=P(("seqhi", "seqlo"), None), check_vma=False
    )
```

```python
import functools

import jax
import jax.numpy as jnp
from jax import lax
from jax.experimental import pallas as pl
from jax.experimental.pallas import tpu as pltpu
from jax.sharding import PartitionSpec as P

HI_LAYERS = 4
NORM_EPS = 1e-05
GELU_SCALE = 0.7978845608028654
GELU_CUBE = 0.044715


def split_high_low(x):
    high = x.astype(jnp.bfloat16)
    return high, (x - high.astype(jnp.float32)).astype(jnp.bfloat16)


def dot(a, b):
    return jnp.dot(a, b, preferred_element_type=jnp.float32)


def dot_split(x, w_high, w_low):
    rows = x.shape[0]
    x_high, x_low = split_high_low(x)
    both = dot(jnp.concatenate([x_high, x_low], axis=0), w_high)
    return both[:rows] + (both[rows:] + dot(x_high, w_low))


def gelu(x):
    half = 0.5 * x
    return half + half * jnp.tanh(x * (GELU_SCALE + (GELU_SCALE * GELU_CUBE) * (x * x)))


def switch_unit(pair, gain, bias, gate, w_in, w_out, hidden_block, out_ready):
    center = pair - jnp.mean(pair, axis=-1, keepdims=True)
    spread = jnp.mean(center * center, axis=-1, keepdims=True)
    normed = center * lax.rsqrt(spread + NORM_EPS) * gain
    out = gate * pair
    in_high, in_low = w_in
    out_high, out_low = w_out
    hidden_count = in_high.shape[1]
    blocks = [slice(c, c + hidden_block) for c in range(0, hidden_count, hidden_block)]

    def enter(cols):
        return dot_split(normed, in_high[:, cols], in_low[:, cols]) + bias[:, cols]

    ahead = enter(blocks[0])
    for number, cols in enumerate(blocks):
        entered = ahead
        if number + 1 < len(blocks):
            ahead = enter(blocks[number + 1])
        hidden = gelu(entered)
        if number == 0:
            out_ready()
        out = out + dot_split(hidden, out_high[cols, :], out_low[cols, :])
    return out


def layers_kernel(
    first, distances, hidden_block,
    x_ref, gain_ref, bias_ref, gate_ref, in_high_ref, in_low_ref, out_high_hbm, out_low_hbm,
    y_ref, out_high_ref, out_low_ref, copied,
):
    copies = [
        pltpu.make_async_copy(out_high_hbm, out_high_ref, copied.at[0]),
        pltpu.make_async_copy(out_low_hbm, out_low_ref, copied.at[1]),
    ]
    for copy in copies:
        copy.start()

    def wait_copies():
        for copy in copies:
            copy.wait()

    rows, width = x_ref.shape
    states = x_ref[...]
    for step, distance in enumerate(distances):
        k = first + step
        groups = rows // (2 * distance)
        grouped = states.reshape(groups, 2, distance, width)
        pair = jnp.concatenate(
            [grouped[:, 0].reshape(-1, width), grouped[:, 1].reshape(-1, width)], axis=-1
        )
        out = switch_unit(
            pair,
            gain_ref[k : k + 1, :],
            bias_ref[k : k + 1, :],
            jax.nn.sigmoid(gate_ref[k : k + 1, :]),
            (in_high_ref, in_low_ref),
            (out_high_ref, out_low_ref),
            hidden_block,
            wait_copies if step == 0 else lambda: None,
        )
        shape = (groups, 1, distance, width)
        states = jnp.concatenate(
            [out[:, :width].reshape(shape), out[:, width:].reshape(shape)], axis=1
        ).reshape(rows, width)
    y_ref[...] = states


def run_layers(states, first, distances, params, name):
    rows, width = states.shape
    hidden = params[1].shape[1]
    kernel = functools.partial(layers_kernel, first, distances, min(hidden, 256))
    vmem = pl.BlockSpec(memory_space=pltpu.VMEM)
    return pl.pallas_call(
        kernel,
        out_shape=jax.ShapeDtypeStruct((rows, width), jnp.float32),
        in_specs=[vmem] * 6 + [pl.BlockSpec(memory_space=pl.ANY)] * 2,
        out_specs=vmem,
        scratch_shapes=[
            pltpu.VMEM(params[-2].shape, params[-2].dtype),
            pltpu.VMEM(params[-1].shape, params[-1].dtype),
            pltpu.SemaphoreType.DMA((2,)),
        ],
        compiler_params=pltpu.CompilerParams(vmem_limit_bytes=60 * 2**20),
        name=name,
    )(states, *params)


def all_to_all(x, axes):
    return lax.all_to_all(x, axes, split_axis=0, concat_axis=0, tiled=True)


def body(features, norm_gain, bias_hidden, gate_logit, w_in, w_out):
    rows = features.shape[0]
    high_count = lax.axis_size("seqhi")
    low_count = lax.axis_size("seqlo")
    high_bits = high_count.bit_length() - 1
    low_bits = low_count.bit_length() - 1
    layer_total = norm_gain.shape[0]

    def parts(w):
        high = lax.reduce_precision(w, exponent_bits=8, mantissa_bits=7)
        return high.astype(jnp.bfloat16), (w - high).astype(jnp.bfloat16)

    params = (norm_gain, bias_hidden, gate_logit, *parts(w_in), *parts(w_out))
    if rows % (8 * high_count * low_count) == 0:
        block = rows // (high_count * low_count)
        distances = [block * 2 ** (k % high_bits) for k in range(HI_LAYERS)]
        distances += [
            block * high_count * 2 ** (j % low_bits) for j in range(layer_total - HI_LAYERS)
        ]
        states = all_to_all(features, ("seqlo", "seqhi"))
        states = run_layers(states, 0, distances, params, "all_layers")
        return all_to_all(states, ("seqlo", "seqhi"))
    high_distances = [rows // high_count * 2 ** (k % high_bits) for k in range(HI_LAYERS)]
    low_distances = [rows // low_count * 2 ** (j % low_bits) for j in range(layer_total - HI_LAYERS)]
    states = all_to_all(features, "seqhi")
    states = run_layers(states, 0, high_distances, params, "high_layers")
    states = all_to_all(states, "seqhi")
    states = all_to_all(states, "seqlo")
    states = run_layers(states, HI_LAYERS, low_distances, params, "low_layers")
    return all_to_all(states, "seqlo")


def solution(mesh):
    placed = (P(("seqhi", "seqlo"), None), P(), P(), P(), P(), P())
    return jax.shard_map(
        body, mesh=mesh, in_specs=placed, out_specs=P(("seqhi", "seqlo"), None), check_vma=False
    )
```

```python
import functools

import jax
import jax.numpy as jnp
from jax import lax
from jax.experimental import pallas as pl
from jax.experimental.pallas import tpu as pltpu
from jax.sharding import PartitionSpec as P

HI_LAYERS = 4
NORM_EPS = 1e-05
GELU_SCALE = 0.7978845608028654
GELU_CUBE = 0.044715


def split_high_low(x):
    high = x.astype(jnp.bfloat16)
    return high, (x - high.astype(jnp.float32)).astype(jnp.bfloat16)


def dot(a, b):
    return jnp.dot(a, b, preferred_element_type=jnp.float32)


def dot_parts(x_high, x_low, w_high, w_low):
    rows = x_high.shape[0]
    both = dot(jnp.concatenate([x_high, x_low], axis=0), w_high)
    return both[:rows] + (both[rows:] + dot(x_high, w_low))


def dot_split(x, w_high, w_low):
    return dot_parts(*split_high_low(x), w_high, w_low)


def gelu(x):
    half = 0.5 * x
    return half + half * jnp.tanh(x * (GELU_SCALE + (GELU_SCALE * GELU_CUBE) * (x * x)))


def switch_unit(pair, gain, bias, gate, w_in, w_out, hidden_block, out_ready):
    center = pair - jnp.mean(pair, axis=-1, keepdims=True)
    spread = jnp.mean(center * center, axis=-1, keepdims=True)
    normed = center * lax.rsqrt(spread + NORM_EPS) * gain
    out = gate * pair
    in_high, in_low = w_in
    out_high, out_low = w_out
    hidden_count = in_high.shape[1]
    blocks = [slice(c, c + hidden_block) for c in range(0, hidden_count, hidden_block)]

    parts = []
    for cols in blocks:
        entered = dot_split(normed, in_high[:, cols], in_low[:, cols]) + bias[:, cols]
        parts.append(split_high_low(gelu(entered)))
    high = jnp.concatenate([part[0] for part in parts], axis=1)
    low = jnp.concatenate([part[1] for part in parts], axis=1)
    out_ready()
    return out + dot_parts(high, low, out_high[...], out_low[...])


def layers_kernel(
    first, distances, hidden_block,
    x_ref, gain_ref, bias_ref, gate_ref, in_high_ref, in_low_ref, out_high_any, out_low_any,
    y_ref, out_high_ref, out_low_ref, copied,
):
    copies = [
        pltpu.make_async_copy(out_high_any, out_high_ref, copied.at[0]),
        pltpu.make_async_copy(out_low_any, out_low_ref, copied.at[1]),
    ]
    for copy in copies:
        copy.start()

    def wait_copies():
        for copy in copies:
            copy.wait()

    rows, width = x_ref.shape
    states = x_ref[...]
    for step, distance in enumerate(distances):
        k = first + step
        groups = rows // (2 * distance)
        grouped = states.reshape(groups, 2, distance, width)
        pair = jnp.concatenate(
            [grouped[:, 0].reshape(-1, width), grouped[:, 1].reshape(-1, width)], axis=-1
        )
        out = switch_unit(
            pair,
            gain_ref[k : k + 1, :],
            bias_ref[k : k + 1, :],
            jax.nn.sigmoid(gate_ref[k : k + 1, :]),
            (in_high_ref, in_low_ref),
            (out_high_ref, out_low_ref),
            hidden_block,
            wait_copies if step == 0 else lambda: None,
        )
        shape = (groups, 1, distance, width)
        states = jnp.concatenate(
            [out[:, :width].reshape(shape), out[:, width:].reshape(shape)], axis=1
        ).reshape(rows, width)
    y_ref[...] = states


def run_layers(states, first, distances, params, name):
    rows, width = states.shape
    hidden = params[1].shape[1]
    kernel = functools.partial(layers_kernel, first, distances, min(hidden, 256))
    vmem = pl.BlockSpec(memory_space=pltpu.VMEM)
    return pl.pallas_call(
        kernel,
        out_shape=jax.ShapeDtypeStruct((rows, width), jnp.float32),
        in_specs=[vmem] * 6 + [pl.BlockSpec(memory_space=pl.ANY)] * 2,
        out_specs=vmem,
        scratch_shapes=[
            pltpu.VMEM(params[-2].shape, params[-2].dtype),
            pltpu.VMEM(params[-1].shape, params[-1].dtype),
            pltpu.SemaphoreType.DMA((2,)),
        ],
        compiler_params=pltpu.CompilerParams(vmem_limit_bytes=51 * 2**20),
        name=name,
    )(states, *params)


def all_to_all(x, axes):
    return lax.all_to_all(x, axes, split_axis=0, concat_axis=0, tiled=True)


def body(features, norm_gain, bias_hidden, gate_logit, w_in, w_out):
    rows = features.shape[0]
    high_count = lax.axis_size("seqhi")
    low_count = lax.axis_size("seqlo")
    high_bits = high_count.bit_length() - 1
    low_bits = low_count.bit_length() - 1
    layer_total = norm_gain.shape[0]

    def parts(w):
        high = lax.reduce_precision(w, exponent_bits=8, mantissa_bits=7)
        return high.astype(jnp.bfloat16), (w - high).astype(jnp.bfloat16)

    params = (norm_gain, bias_hidden, gate_logit, *parts(w_in), *parts(w_out))
    if rows % (8 * high_count * low_count) == 0:
        block = rows // (high_count * low_count)
        distances = [block * low_count * 2 ** (k % high_bits) for k in range(HI_LAYERS)]
        distances += [block * 2 ** (j % low_bits) for j in range(layer_total - HI_LAYERS)]
        states = all_to_all(features, ("seqhi", "seqlo"))
        states = run_layers(states, 0, distances, params, "all_layers")
        return all_to_all(states, ("seqhi", "seqlo"))
    high_distances = [rows // high_count * 2 ** (k % high_bits) for k in range(HI_LAYERS)]
    low_distances = [rows // low_count * 2 ** (j % low_bits) for j in range(layer_total - HI_LAYERS)]
    states = all_to_all(features, "seqhi")
    states = run_layers(states, 0, high_distances, params, "high_layers")
    states = all_to_all(states, "seqhi")
    states = all_to_all(states, "seqlo")
    states = run_layers(states, HI_LAYERS, low_distances, params, "low_layers")
    return all_to_all(states, "seqlo")


def solution(mesh):
    placed = (P(("seqhi", "seqlo"), None), P(), P(), P(), P(), P())
    return jax.shard_map(
        body, mesh=mesh, in_specs=placed, out_specs=P(("seqhi", "seqlo"), None), check_vma=False
    )
```

```python
import functools

import jax
import jax.numpy as jnp
from jax import lax
from jax.experimental import pallas as pl
from jax.experimental.pallas import tpu as pltpu
from jax.sharding import PartitionSpec as P

HI_LAYERS = 4
NORM_EPS = 1e-05
GELU_SCALE = 0.7978845608028654
GELU_CUBE = 0.044715


def split_high_low(x):
    high = x.astype(jnp.bfloat16)
    return high, (x - high.astype(jnp.float32)).astype(jnp.bfloat16)


def gelu(x):
    half = 0.5 * x
    return half + half * jnp.tanh(x * (GELU_SCALE + (GELU_SCALE * GELU_CUBE) * (x * x)))


class Units:
    def __init__(self, sequences):
        self.sequences = [iter(sequence) for sequence in sequences]
        self.register = [0] * len(sequences)
        for unit in range(len(sequences)):
            self.push(unit, 0)

    def push(self, unit, register):
        tile = next(self.sequences[unit], None)
        if tile is not None:
            pltpu.matmul_push_rhs(tile(), register, unit)

    def multiply(self, unit, acc, operands):
        register = self.register[unit]
        self.register[unit] = 1 - register
        self.push(unit, 1 - register)
        for number, operand in enumerate(operands):
            pltpu.matmul_acc_lhs(acc, operand, load_staged_rhs=register if number == 0 else None)


def layers_kernel(
    first, distances, units_count, tile, acc_types,
    x_ref, gain_ref, bias_ref, gate_ref, in_high_ref, in_low_ref, out_high_any, out_low_any,
    y_ref, out_high_ref, out_low_ref, copied,
):
    pl.run_scoped(
        functools.partial(
            layers_body, first, distances, units_count, tile,
            x_ref, gain_ref, bias_ref, gate_ref, in_high_ref, in_low_ref, out_high_any, out_low_any,
            y_ref, out_high_ref, out_low_ref, copied,
        ),
        *acc_types,
    )


def layers_body(
    first, distances, units_count, tile,
    x_ref, gain_ref, bias_ref, gate_ref, in_high_ref, in_low_ref, out_high_any, out_low_any,
    y_ref, out_high_ref, out_low_ref, copied, *accs,
):
    copies = [
        pltpu.make_async_copy(out_high_any, out_high_ref, copied.at[0]),
        pltpu.make_async_copy(out_low_any, out_low_ref, copied.at[1]),
    ]
    for copy in copies:
        copy.start()
    pending = list(copies)

    rows, width = x_ref.shape
    pair_width, hidden_count = in_high_ref.shape
    in_tiles, hidden_tiles, out_tiles = pair_width // tile, hidden_count // tile, pair_width // tile
    hidden_accs, out_accs = accs[:hidden_tiles], accs[hidden_tiles:]

    def span(index):
        return slice(index * tile, (index + 1) * tile)

    def loader(ref, row, col, late):
        def load():
            while late and pending:
                pending.pop().wait()
            return ref[span(row), span(col)]
        return load

    def sequence(unit):
        for _ in distances:
            for col in range(unit, hidden_tiles, units_count):
                for row in range(in_tiles):
                    yield loader(in_high_ref, row, col, False)
                    yield loader(in_low_ref, row, col, False)
            for row in range(hidden_tiles):
                for col in range(unit, out_tiles, units_count):
                    yield loader(out_high_ref, row, col, True)
                    yield loader(out_low_ref, row, col, True)

    units = Units([sequence(unit) for unit in range(units_count)])
    states = x_ref[...]
    for step, distance in enumerate(distances):
        k = first + step
        groups = rows // (2 * distance)
        grouped = states.reshape(groups, 2, distance, width)
        pair = jnp.concatenate(
            [grouped[:, 0].reshape(-1, width), grouped[:, 1].reshape(-1, width)], axis=-1
        )
        center = pair - jnp.mean(pair, axis=-1, keepdims=True)
        spread = jnp.mean(center * center, axis=-1, keepdims=True)
        normed = center * lax.rsqrt(spread + NORM_EPS) * gain_ref[k : k + 1, :]
        high, low = split_high_low(normed)
        for start in range(0, hidden_tiles, units_count):
            for row in range(in_tiles):
                x_high, x_low = high[:, span(row)], low[:, span(row)]
                for operands in ((x_high, x_low), (x_high,)):
                    for unit in range(units_count):
                        units.multiply(unit, hidden_accs[start + unit], operands)
        for row in range(hidden_tiles):
            entered = pltpu.matmul_pop(hidden_accs[row]) + bias_ref[k : k + 1, span(row)]
            h_high, h_low = split_high_low(gelu(entered))
            for start in range(0, out_tiles, units_count):
                for operands in ((h_high, h_low), (h_high,)):
                    for unit in range(units_count):
                        units.multiply(unit, out_accs[start + unit], operands)
        mixed = jnp.concatenate([pltpu.matmul_pop(acc) for acc in out_accs], axis=1)
        out = jax.nn.sigmoid(gate_ref[k : k + 1, :]) * pair + mixed
        shape = (groups, 1, distance, width)
        states = jnp.concatenate(
            [out[:, :width].reshape(shape), out[:, width:].reshape(shape)], axis=1
        ).reshape(rows, width)
    y_ref[...] = states


def run_layers(states, first, distances, params, name):
    rows, width = states.shape
    pair_width, hidden = params[3].shape
    info = pltpu.get_tpu_info()
    units, tile = info.num_mxus, info.mxu_column_size
    acc_types = [
        pltpu.ACC(i % units)((rows // 2, tile), jnp.float32)
        for count in (hidden // tile, pair_width // tile)
        for i in range(count)
    ]
    kernel = functools.partial(layers_kernel, first, distances, units, tile, acc_types)
    vmem = pl.BlockSpec(memory_space=pltpu.VMEM)
    return pl.pallas_call(
        kernel,
        out_shape=jax.ShapeDtypeStruct((rows, width), jnp.float32),
        in_specs=[vmem] * 6 + [pl.BlockSpec(memory_space=pl.ANY)] * 2,
        out_specs=vmem,
        scratch_shapes=[
            pltpu.VMEM(params[-2].shape, params[-2].dtype),
            pltpu.VMEM(params[-1].shape, params[-1].dtype),
            pltpu.SemaphoreType.DMA((2,)),
        ],
        compiler_params=pltpu.CompilerParams(vmem_limit_bytes=51 * 2**20),
        name=name,
    )(states, *params)


def all_to_all(x, axes):
    return lax.all_to_all(x, axes, split_axis=0, concat_axis=0, tiled=True)


def body(features, norm_gain, bias_hidden, gate_logit, w_in, w_out):
    rows = features.shape[0]
    high_count = lax.axis_size("seqhi")
    low_count = lax.axis_size("seqlo")
    high_bits = high_count.bit_length() - 1
    low_bits = low_count.bit_length() - 1
    layer_total = norm_gain.shape[0]

    def parts(w):
        high = lax.reduce_precision(w, exponent_bits=8, mantissa_bits=7)
        return high.astype(jnp.bfloat16), (w - high).astype(jnp.bfloat16)

    params = (norm_gain, bias_hidden, gate_logit, *parts(w_in), *parts(w_out))
    if rows % (8 * high_count * low_count) == 0:
        block = rows // (high_count * low_count)
        distances = [block * low_count * 2 ** (k % high_bits) for k in range(HI_LAYERS)]
        distances += [block * 2 ** (j % low_bits) for j in range(layer_total - HI_LAYERS)]
        states = all_to_all(features, ("seqhi", "seqlo"))
        states = run_layers(states, 0, distances, params, "all_layers")
        return all_to_all(states, ("seqhi", "seqlo"))
    high_distances = [rows // high_count * 2 ** (k % high_bits) for k in range(HI_LAYERS)]
    low_distances = [rows // low_count * 2 ** (j % low_bits) for j in range(layer_total - HI_LAYERS)]
    states = all_to_all(features, "seqhi")
    states = run_layers(states, 0, high_distances, params, "high_layers")
    states = all_to_all(states, "seqhi")
    states = all_to_all(states, "seqlo")
    states = run_layers(states, HI_LAYERS, low_distances, params, "low_layers")
    return all_to_all(states, "seqlo")


def solution(mesh):
    placed = (P(("seqhi", "seqlo"), None), P(), P(), P(), P(), P())
    return jax.shard_map(
        body, mesh=mesh, in_specs=placed, out_specs=P(("seqhi", "seqlo"), None), check_vma=False
    )
```

```python
import functools

import jax
import jax.numpy as jnp
from jax import lax
from jax.experimental import pallas as pl
from jax.experimental.pallas import tpu as pltpu
from jax.sharding import PartitionSpec as P

HI_LAYERS = 4
NORM_EPS = 1e-05
CHUNK_ROWS = 32
GELU_SCALE = 0.7978845608028654
GELU_CUBE = 0.044715


def split_high_low(x):
    high = x.astype(jnp.bfloat16)
    return high, (x - high.astype(jnp.float32)).astype(jnp.bfloat16)


def gelu(x):
    half = 0.5 * x
    return half + half * jnp.tanh(x * (GELU_SCALE + (GELU_SCALE * GELU_CUBE) * (x * x)))


class Units:
    def __init__(self, sequences):
        self.sequences = [iter(sequence) for sequence in sequences]
        self.register = 0
        self.push(0)

    def push(self, register):
        for unit, sequence in enumerate(self.sequences):
            tile = next(sequence, None)
            if tile is not None:
                pltpu.matmul_push_rhs(tile(), register, unit)

    def multiply(self, feed):
        register = self.register
        self.register = 1 - register
        self.push(1 - register)
        fresh = [True] * len(self.sequences)
        for unit, acc, operand in feed:
            pltpu.matmul_acc_lhs(acc, operand, load_staged_rhs=register if fresh[unit] else None)
            fresh[unit] = False


def layers_kernel(
    first, distances, units_count, tile, acc_types,
    x_ref, gain_ref, bias_ref, gate_ref, in_high_ref, in_low_ref, out_high_any, out_low_any,
    y_ref, out_high_ref, out_low_ref, copied,
):
    pl.run_scoped(
        functools.partial(
            layers_body, first, distances, units_count, tile,
            x_ref, gain_ref, bias_ref, gate_ref, in_high_ref, in_low_ref, out_high_any, out_low_any,
            y_ref, out_high_ref, out_low_ref, copied,
        ),
        *acc_types,
    )


def layers_body(
    first, distances, units_count, tile,
    x_ref, gain_ref, bias_ref, gate_ref, in_high_ref, in_low_ref, out_high_any, out_low_any,
    y_ref, out_high_ref, out_low_ref, copied, *accs,
):
    copies = [
        pltpu.make_async_copy(out_high_any, out_high_ref, copied.at[0]),
        pltpu.make_async_copy(out_low_any, out_low_ref, copied.at[1]),
    ]
    for copy in copies:
        copy.start()
    pending = list(copies)

    rows, width = x_ref.shape
    pair_width, hidden_count = in_high_ref.shape
    in_tiles, hidden_tiles, out_tiles = pair_width // tile, hidden_count // tile, pair_width // tile
    hidden_accs, out_accs = accs[:hidden_tiles], accs[hidden_tiles:]

    def span(index):
        return slice(index * tile, (index + 1) * tile)

    def loader(ref, row, col, late):
        def load():
            while late and pending:
                pending.pop().wait()
            return ref[span(row), span(col)]
        return load

    def sequence(unit):
        for _ in distances:
            for col in range(unit, hidden_tiles, units_count):
                for row in range(in_tiles):
                    yield loader(in_high_ref, row, col, False)
                    yield loader(in_low_ref, row, col, False)
            for row in range(hidden_tiles):
                for col in range(unit, out_tiles, units_count):
                    yield loader(out_high_ref, row, col, True)
                    yield loader(out_low_ref, row, col, True)

    units = Units([sequence(unit) for unit in range(units_count)])
    chunks = len(hidden_accs[0])
    chunk = rows // 2 // chunks
    hidden_groups = [
        range(start, start + units_count) for start in range(0, hidden_tiles, units_count)
    ]
    out_groups = [range(start, start + units_count) for start in range(0, out_tiles, units_count)]

    def pair_spans(number, distance):
        piece = min(chunk, distance)
        for index in range(number * chunk, (number + 1) * chunk, piece):
            start = index // distance * 2 * distance + index % distance
            yield start, piece

    def pair_rows(ref, number, distance):
        spans = list(pair_spans(number, distance))
        sides = [
            jnp.concatenate([ref[s + side : s + side + n, :] for s, n in spans], axis=0)
            for side in (0, distance)
        ]
        return jnp.concatenate(sides, axis=1)

    def layer(k, distance, source):
        normed, hidden = {}, {}

        def norm(number):
            if number not in normed:
                pair = pair_rows(source, number, distance)
                center = pair - jnp.mean(pair, axis=-1, keepdims=True)
                spread = jnp.mean(center * center, axis=-1, keepdims=True)
                normed[number] = split_high_low(
                    center * lax.rsqrt(spread + NORM_EPS) * gain_ref[k : k + 1, :]
                )
            return normed[number]

        def activate(row, number):
            if (row, number) not in hidden:
                entered = pltpu.matmul_pop(hidden_accs[row][number])
                hidden[row, number] = split_high_low(gelu(entered + bias_ref[k : k + 1, span(row)]))
            return hidden[row, number]

        def feed(group, accs, operand_of, low_too, tasks):
            for number in range(chunks):
                operands = operand_of(number)
                for operand in operands if low_too else operands[:1]:
                    for unit, col in enumerate(group):
                        yield unit, accs[col][number], operand
                if number % 2 and tasks:
                    activate(*tasks.pop(0))

        def normed_part(row):
            return lambda number: [part[:, span(row)] for part in norm(number)]

        tasks = []
        for group in hidden_groups:
            for row in range(in_tiles):
                for low_too in (True, False):
                    units.multiply(feed(group, hidden_accs, normed_part(row), low_too, tasks))
            tasks += [(row, number) for row in group for number in range(chunks)]
        for row in range(hidden_tiles):
            tasks = [task for task in tasks if task[0] > row or task not in hidden]
            for group in out_groups:
                for low_too in (True, False):
                    units.multiply(
                        feed(group, out_accs, functools.partial(activate, row), low_too, tasks)
                    )
        gate = jax.nn.sigmoid(gate_ref[k : k + 1, :])
        for number in range(chunks):
            mixed = jnp.concatenate([pltpu.matmul_pop(accs[number]) for accs in out_accs], axis=1)
            out = gate * pair_rows(source, number, distance) + mixed
            done = 0
            for start, piece in pair_spans(number, distance):
                block = out[done : done + piece]
                y_ref[start : start + piece, :] = block[:, :width]
                y_ref[start + distance : start + distance + piece, :] = block[:, width:]
                done += piece

    for step, distance in enumerate(distances):
        layer(first + step, distance, x_ref if step == 0 else y_ref)


def run_layers(states, first, distances, params, name):
    rows, width = states.shape
    pair_width, hidden = params[3].shape
    info = pltpu.get_tpu_info()
    units, tile = info.num_mxus, info.mxu_column_size
    chunk = min(rows // 2, CHUNK_ROWS)
    acc_types = [
        [
            pltpu.ACC(i % units)((chunk, tile), jnp.float32)
            for _ in range(rows // 2 // chunk)
        ]
        for count in (hidden // tile, pair_width // tile)
        for i in range(count)
    ]
    kernel = functools.partial(layers_kernel, first, distances, units, tile, acc_types)
    vmem = pl.BlockSpec(memory_space=pltpu.VMEM)
    return pl.pallas_call(
        kernel,
        out_shape=jax.ShapeDtypeStruct((rows, width), jnp.float32),
        in_specs=[vmem] * 6 + [pl.BlockSpec(memory_space=pl.ANY)] * 2,
        out_specs=vmem,
        scratch_shapes=[
            pltpu.VMEM(params[-2].shape, params[-2].dtype),
            pltpu.VMEM(params[-1].shape, params[-1].dtype),
            pltpu.SemaphoreType.DMA((2,)),
        ],
        compiler_params=pltpu.CompilerParams(vmem_limit_bytes=51 * 2**20),
        name=name,
    )(states, *params)


def all_to_all(x, axes):
    return lax.all_to_all(x, axes, split_axis=0, concat_axis=0, tiled=True)


def body(features, norm_gain, bias_hidden, gate_logit, w_in, w_out):
    rows = features.shape[0]
    high_count = lax.axis_size("seqhi")
    low_count = lax.axis_size("seqlo")
    high_bits = high_count.bit_length() - 1
    low_bits = low_count.bit_length() - 1
    layer_total = norm_gain.shape[0]

    def parts(w):
        high = lax.reduce_precision(w, exponent_bits=8, mantissa_bits=7)
        return high.astype(jnp.bfloat16), (w - high).astype(jnp.bfloat16)

    params = (norm_gain, bias_hidden, gate_logit, *parts(w_in), *parts(w_out))
    if rows % (8 * high_count * low_count) == 0:
        block = rows // (high_count * low_count)
        distances = [block * low_count * 2 ** (k % high_bits) for k in range(HI_LAYERS)]
        distances += [block * 2 ** (j % low_bits) for j in range(layer_total - HI_LAYERS)]
        states = all_to_all(features, ("seqhi", "seqlo"))
        states = run_layers(states, 0, distances, params, "all_layers")
        return all_to_all(states, ("seqhi", "seqlo"))
    high_distances = [rows // high_count * 2 ** (k % high_bits) for k in range(HI_LAYERS)]
    low_distances = [rows // low_count * 2 ** (j % low_bits) for j in range(layer_total - HI_LAYERS)]
    states = all_to_all(features, "seqhi")
    states = run_layers(states, 0, high_distances, params, "high_layers")
    states = all_to_all(states, "seqhi")
    states = all_to_all(states, "seqlo")
    states = run_layers(states, HI_LAYERS, low_distances, params, "low_layers")
    return all_to_all(states, "seqlo")


def solution(mesh):
    placed = (P(("seqhi", "seqlo"), None), P(), P(), P(), P(), P())
    return jax.shard_map(
        body, mesh=mesh, in_specs=placed, out_specs=P(("seqhi", "seqlo"), None), check_vma=False
    )
```

```python
import functools

import jax
import jax.numpy as jnp
from jax import lax
from jax.experimental import pallas as pl
from jax.experimental.pallas import tpu as pltpu
from jax.sharding import PartitionSpec as P

HI_LAYERS = 4
NORM_EPS = 1e-05
GELU_SCALE = 0.7978845608028654
GELU_CUBE = 0.044715


def split_high_low(x):
    high = x.astype(jnp.bfloat16)
    return high, (x - high.astype(jnp.float32)).astype(jnp.bfloat16)


def dot(a, b):
    return jnp.dot(a, b, preferred_element_type=jnp.float32)


def dot_parts(x_high, x_low, w_high, w_low):
    rows = x_high.shape[0]
    both = dot(jnp.concatenate([x_high, x_low], axis=0), w_high)
    return both[:rows] + (both[rows:] + dot(x_high, w_low))


def dot_split(x, w_high, w_low):
    return dot_parts(*split_high_low(x), w_high, w_low)


def gelu(x):
    half = 0.5 * x
    return half + half * jnp.tanh(x * (GELU_SCALE + (GELU_SCALE * GELU_CUBE) * (x * x)))


def switch_unit(pair, gain, bias, gate, w_in, w_out, hidden_block, out_ready):
    center = pair - jnp.mean(pair, axis=-1, keepdims=True)
    spread = jnp.mean(center * center, axis=-1, keepdims=True)
    normed = center * lax.rsqrt(spread + NORM_EPS) * gain
    out = gate * pair
    in_high, in_low = w_in
    out_high, out_low = w_out
    hidden_count = in_high.shape[1]
    blocks = [slice(c, c + hidden_block) for c in range(0, hidden_count, hidden_block)]

    parts = []
    for cols in blocks:
        entered = dot_split(normed, in_high[:, cols], in_low[:, cols]) + bias[:, cols]
        parts.append(split_high_low(gelu(entered)))
    high = jnp.concatenate([part[0] for part in parts], axis=1)
    low = jnp.concatenate([part[1] for part in parts], axis=1)
    out_ready()
    return out + dot_parts(high, low, out_high[...], out_low[...])


def layers_kernel(
    first, distances, hidden_block,
    x_ref, gain_ref, bias_ref, gate_ref, in_high_ref, in_low_ref, out_high_any, out_low_any,
    y_ref, out_high_ref, out_low_ref, copied,
):
    copies = [
        pltpu.make_async_copy(out_high_any, out_high_ref, copied.at[0]),
        pltpu.make_async_copy(out_low_any, out_low_ref, copied.at[1]),
    ]
    for copy in copies:
        copy.start()

    def wait_copies():
        for copy in copies:
            copy.wait()

    rows, width = x_ref.shape
    states = x_ref[...]
    for step, distance in enumerate(distances):
        k = first + step
        groups = rows // (2 * distance)
        grouped = states.reshape(groups, 2, distance, width)
        pair = jnp.concatenate(
            [grouped[:, 0].reshape(-1, width), grouped[:, 1].reshape(-1, width)], axis=-1
        )
        out = switch_unit(
            pair,
            gain_ref[k : k + 1, :],
            bias_ref[k : k + 1, :],
            jax.nn.sigmoid(gate_ref[k : k + 1, :]),
            (in_high_ref, in_low_ref),
            (out_high_ref, out_low_ref),
            hidden_block,
            wait_copies if step == 0 else lambda: None,
        )
        shape = (groups, 1, distance, width)
        states = jnp.concatenate(
            [out[:, :width].reshape(shape), out[:, width:].reshape(shape)], axis=1
        ).reshape(rows, width)
    y_ref[...] = states


def run_layers(states, first, distances, params, name):
    rows, width = states.shape
    hidden = params[1].shape[1]
    kernel = functools.partial(layers_kernel, first, distances, min(hidden, 512))
    vmem = pl.BlockSpec(memory_space=pltpu.VMEM)
    return pl.pallas_call(
        kernel,
        out_shape=jax.ShapeDtypeStruct((rows, width), jnp.float32),
        in_specs=[vmem] * 6 + [pl.BlockSpec(memory_space=pl.ANY)] * 2,
        out_specs=vmem,
        scratch_shapes=[
            pltpu.VMEM(params[-2].shape, params[-2].dtype),
            pltpu.VMEM(params[-1].shape, params[-1].dtype),
            pltpu.SemaphoreType.DMA((2,)),
        ],
        compiler_params=pltpu.CompilerParams(vmem_limit_bytes=51 * 2**20),
        name=name,
    )(states, *params)


def all_to_all(x, axes):
    return lax.all_to_all(x, axes, split_axis=0, concat_axis=0, tiled=True)


def body(features, norm_gain, bias_hidden, gate_logit, w_in, w_out):
    rows = features.shape[0]
    high_count = lax.axis_size("seqhi")
    low_count = lax.axis_size("seqlo")
    high_bits = high_count.bit_length() - 1
    low_bits = low_count.bit_length() - 1
    layer_total = norm_gain.shape[0]

    def parts(w):
        high = lax.reduce_precision(w, exponent_bits=8, mantissa_bits=7)
        return high.astype(jnp.bfloat16), (w - high).astype(jnp.bfloat16)

    params = (norm_gain, bias_hidden, gate_logit, *parts(w_in), *parts(w_out))
    if rows % (8 * high_count * low_count) == 0:
        block = rows // (high_count * low_count)
        distances = [block * low_count * 2 ** (k % high_bits) for k in range(HI_LAYERS)]
        distances += [block * 2 ** (j % low_bits) for j in range(layer_total - HI_LAYERS)]
        states = all_to_all(features, ("seqhi", "seqlo"))
        states = run_layers(states, 0, distances, params, "all_layers")
        return all_to_all(states, ("seqhi", "seqlo"))
    high_distances = [rows // high_count * 2 ** (k % high_bits) for k in range(HI_LAYERS)]
    low_distances = [rows // low_count * 2 ** (j % low_bits) for j in range(layer_total - HI_LAYERS)]
    states = all_to_all(features, "seqhi")
    states = run_layers(states, 0, high_distances, params, "high_layers")
    states = all_to_all(states, "seqhi")
    states = all_to_all(states, "seqlo")
    states = run_layers(states, HI_LAYERS, low_distances, params, "low_layers")
    return all_to_all(states, "seqlo")


def solution(mesh):
    placed = (P(("seqhi", "seqlo"), None), P(), P(), P(), P(), P())
    return jax.shard_map(
        body, mesh=mesh, in_specs=placed, out_specs=P(("seqhi", "seqlo"), None), check_vma=False
    )
```

```python
import functools

import jax
import jax.numpy as jnp
from jax import lax
from jax.experimental import pallas as pl
from jax.experimental.pallas import tpu as pltpu
from jax.sharding import PartitionSpec as P

HI_LAYERS = 4
NORM_EPS = 1e-05
GELU_SCALE = 0.7978845608028654
GELU_CUBE = 0.044715


def split_high_low(x):
    high = x.astype(jnp.bfloat16)
    return high, (x - high.astype(jnp.float32)).astype(jnp.bfloat16)


def dot(a, b):
    return jnp.dot(a, b, preferred_element_type=jnp.float32)


def dot_parts(x_high, x_low, w_high, w_low):
    rows = x_high.shape[0]
    both = dot(jnp.concatenate([x_high, x_low], axis=0), w_high)
    return both[:rows] + (both[rows:] + dot(x_high, w_low))


def gelu(x):
    half = 0.5 * x
    return half + half * jnp.tanh(x * (GELU_SCALE + (GELU_SCALE * GELU_CUBE) * (x * x)))


def switch_unit(pair, gain, bias, gate, w_in, w_out, hidden_block, out_ready):
    center = pair - jnp.mean(pair, axis=-1, keepdims=True)
    spread = jnp.mean(center * center, axis=-1, keepdims=True)
    scale = lax.rsqrt(spread + NORM_EPS)
    scaled = split_high_low(center * gain)
    out = gate * pair
    in_high, in_low = w_in
    out_high, out_low = w_out
    hidden_count = in_high.shape[1]
    blocks = [slice(c, c + hidden_block) for c in range(0, hidden_count, hidden_block)]

    parts = []
    for cols in blocks:
        product = dot_parts(*scaled, in_high[:, cols], in_low[:, cols])
        entered = product * scale + bias[:, cols]
        parts.append(split_high_low(gelu(entered)))
    high = jnp.concatenate([part[0] for part in parts], axis=1)
    low = jnp.concatenate([part[1] for part in parts], axis=1)
    out_ready()
    return out + dot_parts(high, low, out_high[...], out_low[...])


def layers_kernel(
    first, distances, hidden_block,
    x_ref, gain_ref, bias_ref, gate_ref, in_high_ref, in_low_ref, out_high_any, out_low_any,
    y_ref, out_high_ref, out_low_ref, copied,
):
    copies = [
        pltpu.make_async_copy(out_high_any, out_high_ref, copied.at[0]),
        pltpu.make_async_copy(out_low_any, out_low_ref, copied.at[1]),
    ]
    for copy in copies:
        copy.start()

    def wait_copies():
        for copy in copies:
            copy.wait()

    rows, width = x_ref.shape
    states = x_ref[...]
    for step, distance in enumerate(distances):
        k = first + step
        groups = rows // (2 * distance)
        grouped = states.reshape(groups, 2, distance, width)
        pair = jnp.concatenate(
            [grouped[:, 0].reshape(-1, width), grouped[:, 1].reshape(-1, width)], axis=-1
        )
        out = switch_unit(
            pair,
            gain_ref[k : k + 1, :],
            bias_ref[k : k + 1, :],
            jax.nn.sigmoid(gate_ref[k : k + 1, :]),
            (in_high_ref, in_low_ref),
            (out_high_ref, out_low_ref),
            hidden_block,
            wait_copies if step == 0 else lambda: None,
        )
        shape = (groups, 1, distance, width)
        states = jnp.concatenate(
            [out[:, :width].reshape(shape), out[:, width:].reshape(shape)], axis=1
        ).reshape(rows, width)
    y_ref[...] = states


def run_layers(states, first, distances, params, name):
    rows, width = states.shape
    hidden = params[1].shape[1]
    kernel = functools.partial(layers_kernel, first, distances, min(hidden, 512))
    vmem = pl.BlockSpec(memory_space=pltpu.VMEM)
    return pl.pallas_call(
        kernel,
        out_shape=jax.ShapeDtypeStruct((rows, width), jnp.float32),
        in_specs=[vmem] * 6 + [pl.BlockSpec(memory_space=pl.ANY)] * 2,
        out_specs=vmem,
        scratch_shapes=[
            pltpu.VMEM(params[-2].shape, params[-2].dtype),
            pltpu.VMEM(params[-1].shape, params[-1].dtype),
            pltpu.SemaphoreType.DMA((2,)),
        ],
        compiler_params=pltpu.CompilerParams(vmem_limit_bytes=51 * 2**20),
        name=name,
    )(states, *params)


def all_to_all(x, axes):
    return lax.all_to_all(x, axes, split_axis=0, concat_axis=0, tiled=True)


def body(features, norm_gain, bias_hidden, gate_logit, w_in, w_out):
    rows = features.shape[0]
    high_count = lax.axis_size("seqhi")
    low_count = lax.axis_size("seqlo")
    high_bits = high_count.bit_length() - 1
    low_bits = low_count.bit_length() - 1
    layer_total = norm_gain.shape[0]

    def parts(w):
        high = lax.reduce_precision(w, exponent_bits=8, mantissa_bits=7)
        return high.astype(jnp.bfloat16), (w - high).astype(jnp.bfloat16)

    params = (norm_gain, bias_hidden, gate_logit, *parts(w_in), *parts(w_out))
    if rows % (8 * high_count * low_count) == 0:
        block = rows // (high_count * low_count)
        distances = [block * low_count * 2 ** (k % high_bits) for k in range(HI_LAYERS)]
        distances += [block * 2 ** (j % low_bits) for j in range(layer_total - HI_LAYERS)]
        states = all_to_all(features, ("seqhi", "seqlo"))
        states = run_layers(states, 0, distances, params, "all_layers")
        return all_to_all(states, ("seqhi", "seqlo"))
    high_distances = [rows // high_count * 2 ** (k % high_bits) for k in range(HI_LAYERS)]
    low_distances = [rows // low_count * 2 ** (j % low_bits) for j in range(layer_total - HI_LAYERS)]
    states = all_to_all(features, "seqhi")
    states = run_layers(states, 0, high_distances, params, "high_layers")
    states = all_to_all(states, "seqhi")
    states = all_to_all(states, "seqlo")
    states = run_layers(states, HI_LAYERS, low_distances, params, "low_layers")
    return all_to_all(states, "seqlo")


def solution(mesh):
    placed = (P(("seqhi", "seqlo"), None), P(), P(), P(), P(), P())
    return jax.shard_map(
        body, mesh=mesh, in_specs=placed, out_specs=P(("seqhi", "seqlo"), None), check_vma=False
    )
```

```python
import functools

import jax
import jax.numpy as jnp
from jax import lax
from jax.experimental import pallas as pl
from jax.experimental.pallas import tpu as pltpu
from jax.sharding import PartitionSpec as P

HI_LAYERS = 4
NORM_EPS = 1e-05
GELU_SCALE = 0.7978845608028654
GELU_CUBE = 0.044715


def split_high_low(x):
    high = x.astype(jnp.bfloat16)
    return high, (x - high.astype(jnp.float32)).astype(jnp.bfloat16)


def gelu(x):
    half = 0.5 * x
    return half + half * jnp.tanh(x * (GELU_SCALE + (GELU_SCALE * GELU_CUBE) * (x * x)))


class Units:
    def __init__(self, sequences):
        self.sequences = [iter(sequence) for sequence in sequences]
        self.register = [0] * len(sequences)
        for unit in range(len(sequences)):
            self.push(unit, 0)

    def push(self, unit, register):
        tile = next(self.sequences[unit], None)
        if tile is not None:
            pltpu.matmul_push_rhs(tile(), register, unit)

    def multiply(self, unit, acc, operands):
        register = self.register[unit]
        self.register[unit] = 1 - register
        self.push(unit, 1 - register)
        for number, operand in enumerate(operands):
            pltpu.matmul_acc_lhs(acc, operand, load_staged_rhs=register if number == 0 else None)


def layers_kernel(
    first, distances, units_count, tile, acc_types,
    x_ref, gain_ref, bias_ref, gate_ref, in_high_ref, in_low_ref, out_high_any, out_low_any,
    y_ref, out_high_ref, out_low_ref, copied,
):
    pl.run_scoped(
        functools.partial(
            layers_body, first, distances, units_count, tile,
            x_ref, gain_ref, bias_ref, gate_ref, in_high_ref, in_low_ref, out_high_any, out_low_any,
            y_ref, out_high_ref, out_low_ref, copied,
        ),
        *acc_types,
    )


def layers_body(
    first, distances, units_count, tile,
    x_ref, gain_ref, bias_ref, gate_ref, in_high_ref, in_low_ref, out_high_any, out_low_any,
    y_ref, out_high_ref, out_low_ref, copied, *accs,
):
    copies = [
        pltpu.make_async_copy(out_high_any, out_high_ref, copied.at[0]),
        pltpu.make_async_copy(out_low_any, out_low_ref, copied.at[1]),
    ]
    for copy in copies:
        copy.start()
    pending = list(copies)

    rows, width = x_ref.shape
    pair_width, hidden_count = in_high_ref.shape
    in_tiles, hidden_tiles, out_tiles = pair_width // tile, hidden_count // tile, pair_width // tile
    hidden_accs, out_accs = accs[:hidden_tiles], accs[hidden_tiles:]

    def span(index):
        return slice(index * tile, (index + 1) * tile)

    def loader(ref, row, col, late):
        def load():
            while late and pending:
                pending.pop().wait()
            return ref[span(row), span(col)]
        return load

    def sequence(unit):
        for _ in distances:
            for col in range(unit, hidden_tiles, units_count):
                for row in range(in_tiles):
                    yield loader(in_high_ref, row, col, False)
                    yield loader(in_low_ref, row, col, False)
            for row in range(hidden_tiles):
                for col in range(unit, out_tiles, units_count):
                    yield loader(out_high_ref, row, col, True)
                    yield loader(out_low_ref, row, col, True)

    units = Units([sequence(unit) for unit in range(units_count)])
    states = x_ref[...]
    for step, distance in enumerate(distances):
        k = first + step
        groups = rows // (2 * distance)
        grouped = states.reshape(groups, 2, distance, width)
        pair = jnp.concatenate(
            [grouped[:, 0].reshape(-1, width), grouped[:, 1].reshape(-1, width)], axis=-1
        )
        center = pair - jnp.mean(pair, axis=-1, keepdims=True)
        spread = jnp.mean(center * center, axis=-1, keepdims=True)
        scale = lax.rsqrt(spread + NORM_EPS)
        residual = jax.nn.sigmoid(gate_ref[k : k + 1, :]) * pair
        high, low = split_high_low(center * gain_ref[k : k + 1, :])
        hidden = []

        def activate():
            row = len(hidden)
            if row < hidden_tiles:
                product = pltpu.matmul_pop(hidden_accs[row])
                entered = product * scale + bias_ref[k : k + 1, span(row)]
                hidden.append(split_high_low(gelu(entered)))

        for start in range(0, hidden_tiles, units_count):
            for row in range(in_tiles):
                x_high, x_low = high[:, span(row)], low[:, span(row)]
                for operands in ((x_high, x_low), (x_high,)):
                    for unit in range(units_count):
                        units.multiply(unit, hidden_accs[start + unit], operands)
                if start > 0 and start + units_count >= hidden_tiles and row == 0:
                    activate()
        for row in range(hidden_tiles):
            while len(hidden) < min(row + 2, hidden_tiles):
                activate()
            h_high, h_low = hidden[row]
            for start in range(0, out_tiles, units_count):
                for operands in ((h_high, h_low), (h_high,)):
                    for unit in range(units_count):
                        units.multiply(unit, out_accs[start + unit], operands)
        mixed = jnp.concatenate([pltpu.matmul_pop(acc) for acc in out_accs], axis=1)
        out = residual + mixed
        shape = (groups, 1, distance, width)
        states = jnp.concatenate(
            [out[:, :width].reshape(shape), out[:, width:].reshape(shape)], axis=1
        ).reshape(rows, width)
    y_ref[...] = states


def run_layers(states, first, distances, params, name):
    rows, width = states.shape
    pair_width, hidden = params[3].shape
    info = pltpu.get_tpu_info()
    units, tile = info.num_mxus, info.mxu_column_size
    acc_types = [
        pltpu.ACC(i % units)((rows // 2, tile), jnp.float32)
        for count in (hidden // tile, pair_width // tile)
        for i in range(count)
    ]
    kernel = functools.partial(layers_kernel, first, distances, units, tile, acc_types)
    vmem = pl.BlockSpec(memory_space=pltpu.VMEM)
    return pl.pallas_call(
        kernel,
        out_shape=jax.ShapeDtypeStruct((rows, width), jnp.float32),
        in_specs=[vmem] * 6 + [pl.BlockSpec(memory_space=pl.ANY)] * 2,
        out_specs=vmem,
        scratch_shapes=[
            pltpu.VMEM(params[-2].shape, params[-2].dtype),
            pltpu.VMEM(params[-1].shape, params[-1].dtype),
            pltpu.SemaphoreType.DMA((2,)),
        ],
        compiler_params=pltpu.CompilerParams(vmem_limit_bytes=51 * 2**20),
        name=name,
    )(states, *params)


def all_to_all(x, axes):
    return lax.all_to_all(x, axes, split_axis=0, concat_axis=0, tiled=True)


def body(features, norm_gain, bias_hidden, gate_logit, w_in, w_out):
    rows = features.shape[0]
    high_count = lax.axis_size("seqhi")
    low_count = lax.axis_size("seqlo")
    high_bits = high_count.bit_length() - 1
    low_bits = low_count.bit_length() - 1
    layer_total = norm_gain.shape[0]

    def parts(w):
        high = lax.reduce_precision(w, exponent_bits=8, mantissa_bits=7)
        return high.astype(jnp.bfloat16), (w - high).astype(jnp.bfloat16)

    params = (norm_gain, bias_hidden, gate_logit, *parts(w_in), *parts(w_out))
    if rows % (8 * high_count * low_count) == 0:
        block = rows // (high_count * low_count)
        distances = [block * low_count * 2 ** (k % high_bits) for k in range(HI_LAYERS)]
        distances += [block * 2 ** (j % low_bits) for j in range(layer_total - HI_LAYERS)]
        states = all_to_all(features, ("seqhi", "seqlo"))
        states = run_layers(states, 0, distances, params, "all_layers")
        return all_to_all(states, ("seqhi", "seqlo"))
    high_distances = [rows // high_count * 2 ** (k % high_bits) for k in range(HI_LAYERS)]
    low_distances = [rows // low_count * 2 ** (j % low_bits) for j in range(layer_total - HI_LAYERS)]
    states = all_to_all(features, "seqhi")
    states = run_layers(states, 0, high_distances, params, "high_layers")
    states = all_to_all(states, "seqhi")
    states = all_to_all(states, "seqlo")
    states = run_layers(states, HI_LAYERS, low_distances, params, "low_layers")
    return all_to_all(states, "seqlo")


def solution(mesh):
    placed = (P(("seqhi", "seqlo"), None), P(), P(), P(), P(), P())
    return jax.shard_map(
        body, mesh=mesh, in_specs=placed, out_specs=P(("seqhi", "seqlo"), None), check_vma=False
    )
```

```python
import functools

import jax
import jax.numpy as jnp
from jax import lax
from jax.experimental import pallas as pl
from jax.experimental.pallas import tpu as pltpu
from jax.sharding import PartitionSpec as P

HI_LAYERS = 4
NORM_EPS = 1e-05
GELU_SCALE = 0.7978845608028654
GELU_CUBE = 0.044715


def split_high_low(x):
    high = x.astype(jnp.bfloat16)
    return high, (x - high.astype(jnp.float32)).astype(jnp.bfloat16)


def dot(a, b):
    return jnp.dot(a, b, preferred_element_type=jnp.float32)


def dot_parts(x_high, x_low, w_high, w_low):
    rows = x_high.shape[0]
    both = dot(jnp.concatenate([x_high, x_low], axis=0), w_high)
    return both[:rows] + (both[rows:] + dot(x_high, w_low))


def gelu(x):
    half = 0.5 * x
    return half + half * jnp.tanh(x * (GELU_SCALE + (GELU_SCALE * GELU_CUBE) * (x * x)))


def switch_unit(pair, gain, bias, gate, w_in, w_out, hidden_block, ready):
    center = pair - jnp.mean(pair, axis=-1, keepdims=True)
    spread = jnp.mean(center * center, axis=-1, keepdims=True)
    scale = lax.rsqrt(spread + NORM_EPS)
    scaled = split_high_low(center * gain)
    out = gate * pair
    in_high, in_low = w_in
    out_high, out_low = w_out
    hidden_count = in_high.shape[1]
    blocks = [slice(c, c + hidden_block) for c in range(0, hidden_count, hidden_block)]

    for cols in blocks:
        product = dot_parts(*scaled, in_high[:, cols], in_low[:, cols])
        h_high, h_low = split_high_low(gelu(product * scale + bias[:, cols]))
        ready(out_high)
        both = dot(jnp.concatenate([h_high, h_low], axis=0), out_high[cols, :])
        ready(out_low)
        out = out + (both[: h_high.shape[0]] + (both[h_high.shape[0] :] + dot(h_high, out_low[cols, :])))
    return out


def layers_kernel(
    first, distances, hidden_block,
    x_ref, gain_ref, bias_ref, gate_ref, in_high_ref, in_low_ref, out_high_any, out_low_any,
    y_ref, out_high_ref, out_low_ref, copied,
):
    pending = []
    for number, (source, target) in enumerate(
        [(out_high_any, out_high_ref), (out_low_any, out_low_ref)]
    ):
        copy = pltpu.make_async_copy(source, target, copied.at[number])
        copy.start()
        pending.append((target, copy))

    def ready(ref):
        for target, copy in list(pending):
            if target is ref:
                copy.wait()
                pending.remove((target, copy))

    rows, width = x_ref.shape
    states = x_ref[...]
    for step, distance in enumerate(distances):
        k = first + step
        groups = rows // (2 * distance)
        grouped = states.reshape(groups, 2, distance, width)
        pair = jnp.concatenate(
            [grouped[:, 0].reshape(-1, width), grouped[:, 1].reshape(-1, width)], axis=-1
        )
        out = switch_unit(
            pair,
            gain_ref[k : k + 1, :],
            bias_ref[k : k + 1, :],
            jax.nn.sigmoid(gate_ref[k : k + 1, :]),
            (in_high_ref, in_low_ref),
            (out_high_ref, out_low_ref),
            hidden_block,
            ready,
        )
        shape = (groups, 1, distance, width)
        states = jnp.concatenate(
            [out[:, :width].reshape(shape), out[:, width:].reshape(shape)], axis=1
        ).reshape(rows, width)
    y_ref[...] = states


def run_layers(states, first, distances, params, name):
    rows, width = states.shape
    hidden = params[1].shape[1]
    kernel = functools.partial(layers_kernel, first, distances, min(hidden, 512))
    vmem = pl.BlockSpec(memory_space=pltpu.VMEM)
    return pl.pallas_call(
        kernel,
        out_shape=jax.ShapeDtypeStruct((rows, width), jnp.float32),
        in_specs=[vmem] * 6 + [pl.BlockSpec(memory_space=pl.ANY)] * 2,
        out_specs=vmem,
        scratch_shapes=[
            pltpu.VMEM(params[-2].shape, params[-2].dtype),
            pltpu.VMEM(params[-1].shape, params[-1].dtype),
            pltpu.SemaphoreType.DMA((2,)),
        ],
        compiler_params=pltpu.CompilerParams(vmem_limit_bytes=51 * 2**20),
        name=name,
    )(states, *params)


def all_to_all(x, axes):
    return lax.all_to_all(x, axes, split_axis=0, concat_axis=0, tiled=True)


def body(features, norm_gain, bias_hidden, gate_logit, w_in, w_out):
    rows = features.shape[0]
    high_count = lax.axis_size("seqhi")
    low_count = lax.axis_size("seqlo")
    high_bits = high_count.bit_length() - 1
    low_bits = low_count.bit_length() - 1
    layer_total = norm_gain.shape[0]

    def parts(w):
        high = lax.reduce_precision(w, exponent_bits=8, mantissa_bits=7)
        return high.astype(jnp.bfloat16), (w - high).astype(jnp.bfloat16)

    params = (norm_gain, bias_hidden, gate_logit, *parts(w_in), *parts(w_out))
    if rows % (8 * high_count * low_count) == 0:
        block = rows // (high_count * low_count)
        distances = [block * low_count * 2 ** (k % high_bits) for k in range(HI_LAYERS)]
        distances += [block * 2 ** (j % low_bits) for j in range(layer_total - HI_LAYERS)]
        states = all_to_all(features, ("seqhi", "seqlo"))
        states = run_layers(states, 0, distances, params, "all_layers")
        return all_to_all(states, ("seqhi", "seqlo"))
    high_distances = [rows // high_count * 2 ** (k % high_bits) for k in range(HI_LAYERS)]
    low_distances = [rows // low_count * 2 ** (j % low_bits) for j in range(layer_total - HI_LAYERS)]
    states = all_to_all(features, "seqhi")
    states = run_layers(states, 0, high_distances, params, "high_layers")
    states = all_to_all(states, "seqhi")
    states = all_to_all(states, "seqlo")
    states = run_layers(states, HI_LAYERS, low_distances, params, "low_layers")
    return all_to_all(states, "seqlo")


def solution(mesh):
    placed = (P(("seqhi", "seqlo"), None), P(), P(), P(), P(), P())
    return jax.shard_map(
        body, mesh=mesh, in_specs=placed, out_specs=P(("seqhi", "seqlo"), None), check_vma=False
    )
```

```python
import functools

import jax
import jax.numpy as jnp
from jax import lax
from jax.experimental import pallas as pl
from jax.experimental.pallas import tpu as pltpu
from jax.sharding import PartitionSpec as P

HI_LAYERS = 4
NORM_EPS = 1e-05
GELU_SCALE = 0.7978845608028654
GELU_CUBE = 0.044715


def split_high_low(x):
    high = x.astype(jnp.bfloat16)
    return high, (x - high.astype(jnp.float32)).astype(jnp.bfloat16)


def dot(a, b):
    return jnp.dot(a, b, preferred_element_type=jnp.float32)


def dot_parts(x_high, x_low, w_high, w_low, base=None):
    rows = x_high.shape[0]
    both = dot(jnp.concatenate([x_high, x_low], axis=0), w_high())
    first = both[:rows] if base is None else base + both[:rows]
    return (first + both[rows:]) + dot(x_high, w_low())


def gelu(x):
    half = 0.5 * x
    return half + half * jnp.tanh(x * (GELU_SCALE + (GELU_SCALE * GELU_CUBE) * (x * x)))


def switch_unit(pair, gain, bias, gate, w_in, w_out, hidden_block, load):
    center = pair - jnp.mean(pair, axis=-1, keepdims=True)
    spread = jnp.mean(center * center, axis=-1, keepdims=True)
    scale = lax.rsqrt(spread + NORM_EPS)
    scaled = split_high_low(center * gain)
    in_high, in_low = w_in
    out_high, out_low = w_out
    hidden_count = in_high.shape[1]
    blocks = [slice(c, c + hidden_block) for c in range(0, hidden_count, hidden_block)]

    parts = []
    for cols in blocks:
        product = dot_parts(*scaled, lambda: in_high[:, cols], lambda: in_low[:, cols])
        entered = product * scale + bias[:, cols]
        parts.append(split_high_low(gelu(entered)))
    high = jnp.concatenate([part[0] for part in parts], axis=1)
    low = jnp.concatenate([part[1] for part in parts], axis=1)
    return dot_parts(high, low, lambda: load(out_high), lambda: load(out_low), gate * pair)


def layers_kernel(
    first, distances, hidden_block,
    x_ref, gain_ref, bias_ref, gate_ref, in_high_ref, in_low_ref, out_high_any, out_low_any,
    y_ref, out_high_ref, out_low_ref, copied,
):
    pending = []
    for number, (source, target) in enumerate(
        [(out_high_any, out_high_ref), (out_low_any, out_low_ref)]
    ):
        copy = pltpu.make_async_copy(source, target, copied.at[number])
        copy.start()
        pending.append((target, copy))

    def load(ref):
        for target, copy in list(pending):
            if target is ref:
                copy.wait()
                pending.remove((target, copy))
        return ref[...]

    rows, width = x_ref.shape
    states = x_ref[...]
    for step, distance in enumerate(distances):
        k = first + step
        groups = rows // (2 * distance)
        grouped = states.reshape(groups, 2, distance, width)
        pair = jnp.concatenate(
            [grouped[:, 0].reshape(-1, width), grouped[:, 1].reshape(-1, width)], axis=-1
        )
        out = switch_unit(
            pair,
            gain_ref[k : k + 1, :],
            bias_ref[k : k + 1, :],
            jax.nn.sigmoid(gate_ref[k : k + 1, :]),
            (in_high_ref, in_low_ref),
            (out_high_ref, out_low_ref),
            hidden_block,
            load,
        )
        shape = (groups, 1, distance, width)
        states = jnp.concatenate(
            [out[:, :width].reshape(shape), out[:, width:].reshape(shape)], axis=1
        ).reshape(rows, width)
    y_ref[...] = states


def run_layers(states, first, distances, params, name):
    rows, width = states.shape
    hidden = params[1].shape[1]
    kernel = functools.partial(layers_kernel, first, distances, min(hidden, 512))
    vmem = pl.BlockSpec(memory_space=pltpu.VMEM)
    return pl.pallas_call(
        kernel,
        out_shape=jax.ShapeDtypeStruct((rows, width), jnp.float32),
        in_specs=[vmem] * 6 + [pl.BlockSpec(memory_space=pl.ANY)] * 2,
        out_specs=vmem,
        scratch_shapes=[
            pltpu.VMEM(params[-2].shape, params[-2].dtype),
            pltpu.VMEM(params[-1].shape, params[-1].dtype),
            pltpu.SemaphoreType.DMA((2,)),
        ],
        compiler_params=pltpu.CompilerParams(vmem_limit_bytes=51 * 2**20),
        name=name,
    )(states, *params)


def all_to_all(x, axes):
    return lax.all_to_all(x, axes, split_axis=0, concat_axis=0, tiled=True)


def body(features, norm_gain, bias_hidden, gate_logit, w_in, w_out):
    rows = features.shape[0]
    high_count = lax.axis_size("seqhi")
    low_count = lax.axis_size("seqlo")
    high_bits = high_count.bit_length() - 1
    low_bits = low_count.bit_length() - 1
    layer_total = norm_gain.shape[0]

    def parts(w):
        high = lax.reduce_precision(w, exponent_bits=8, mantissa_bits=7)
        return high.astype(jnp.bfloat16), (w - high).astype(jnp.bfloat16)

    params = (norm_gain, bias_hidden, gate_logit, *parts(w_in), *parts(w_out))
    if rows % (8 * high_count * low_count) == 0:
        block = rows // (high_count * low_count)
        distances = [block * low_count * 2 ** (k % high_bits) for k in range(HI_LAYERS)]
        distances += [block * 2 ** (j % low_bits) for j in range(layer_total - HI_LAYERS)]
        states = all_to_all(features, ("seqhi", "seqlo"))
        states = run_layers(states, 0, distances, params, "all_layers")
        return all_to_all(states, ("seqhi", "seqlo"))
    high_distances = [rows // high_count * 2 ** (k % high_bits) for k in range(HI_LAYERS)]
    low_distances = [rows // low_count * 2 ** (j % low_bits) for j in range(layer_total - HI_LAYERS)]
    states = all_to_all(features, "seqhi")
    states = run_layers(states, 0, high_distances, params, "high_layers")
    states = all_to_all(states, "seqhi")
    states = all_to_all(states, "seqlo")
    states = run_layers(states, HI_LAYERS, low_distances, params, "low_layers")
    return all_to_all(states, "seqlo")


def solution(mesh):
    placed = (P(("seqhi", "seqlo"), None), P(), P(), P(), P(), P())
    return jax.shard_map(
        body, mesh=mesh, in_specs=placed, out_specs=P(("seqhi", "seqlo"), None), check_vma=False
    )
```

```python
import functools

import jax
import jax.numpy as jnp
from jax import lax
from jax.experimental import pallas as pl
from jax.experimental.pallas import tpu as pltpu
from jax.sharding import PartitionSpec as P

HI_LAYERS = 4
NORM_EPS = 1e-05
GELU_SCALE = 0.7978845608028654
GELU_CUBE = 0.044715


def split_high_low(x):
    high = x.astype(jnp.bfloat16)
    return high, (x - high.astype(jnp.float32)).astype(jnp.bfloat16)


def dot(a, b):
    return jnp.dot(a, b, preferred_element_type=jnp.float32)


def dot_parts(x_high, x_low, w_high, w_low, base=None):
    rows = x_high.shape[0]
    both = dot(jnp.concatenate([x_high, x_low], axis=0), w_high())
    first = both[:rows] if base is None else base + both[:rows]
    return (first + both[rows:]) + dot(x_high, w_low())


def gelu(x):
    half = 0.5 * x
    return half + half * jnp.tanh(x * (GELU_SCALE + (GELU_SCALE * GELU_CUBE) * (x * x)))


def switch_unit(pair, gain, bias, gate, w_in, w_out, hidden_block, load):
    center = pair - jnp.mean(pair, axis=-1, keepdims=True)
    spread = jnp.mean(center * center, axis=-1, keepdims=True)
    scale = lax.rsqrt(spread + NORM_EPS)
    scaled = split_high_low(center * gain)
    in_high, in_low = w_in
    out_high, out_low = w_out
    hidden_count = in_high.shape[1]
    blocks = [slice(c, c + hidden_block) for c in range(0, hidden_count, hidden_block)]

    parts = []
    for cols in blocks:
        product = dot_parts(*scaled, lambda: in_high[:, cols], lambda: in_low[:, cols])
        entered = product * scale + bias[:, cols]
        parts.append(split_high_low(gelu(entered)))
    out = gate * pair
    for cols, (high, low) in zip(blocks, parts):
        out = dot_parts(high, low, lambda: load(out_high, cols), lambda: load(out_low, cols), out)
    return out


def layers_kernel(
    first, distances, hidden_block,
    x_ref, gain_ref, bias_ref, gate_ref, in_high_ref, in_low_ref, out_high_any, out_low_any,
    y_ref, out_high_ref, out_low_ref, copied,
):
    pending = []
    for number, (source, target) in enumerate(
        [(out_high_any, out_high_ref), (out_low_any, out_low_ref)]
    ):
        copy = pltpu.make_async_copy(source, target, copied.at[number])
        copy.start()
        pending.append((target, copy))

    def load(ref, depth):
        for target, copy in list(pending):
            if target is ref:
                copy.wait()
                pending.remove((target, copy))
        return ref[depth, :]

    rows, width = x_ref.shape
    states = x_ref[...]
    for step, distance in enumerate(distances):
        k = first + step
        groups = rows // (2 * distance)
        grouped = states.reshape(groups, 2, distance, width)
        pair = jnp.concatenate(
            [grouped[:, 0].reshape(-1, width), grouped[:, 1].reshape(-1, width)], axis=-1
        )
        out = switch_unit(
            pair,
            gain_ref[k : k + 1, :],
            bias_ref[k : k + 1, :],
            jax.nn.sigmoid(gate_ref[k : k + 1, :]),
            (in_high_ref, in_low_ref),
            (out_high_ref, out_low_ref),
            hidden_block,
            load,
        )
        shape = (groups, 1, distance, width)
        states = jnp.concatenate(
            [out[:, :width].reshape(shape), out[:, width:].reshape(shape)], axis=1
        ).reshape(rows, width)
    y_ref[...] = states


def run_layers(states, first, distances, params, name):
    rows, width = states.shape
    hidden = params[1].shape[1]
    kernel = functools.partial(layers_kernel, first, distances, min(hidden, 512))
    vmem = pl.BlockSpec(memory_space=pltpu.VMEM)
    return pl.pallas_call(
        kernel,
        out_shape=jax.ShapeDtypeStruct((rows, width), jnp.float32),
        in_specs=[vmem] * 6 + [pl.BlockSpec(memory_space=pl.ANY)] * 2,
        out_specs=vmem,
        scratch_shapes=[
            pltpu.VMEM(params[-2].shape, params[-2].dtype),
            pltpu.VMEM(params[-1].shape, params[-1].dtype),
            pltpu.SemaphoreType.DMA((2,)),
        ],
        compiler_params=pltpu.CompilerParams(vmem_limit_bytes=51 * 2**20),
        name=name,
    )(states, *params)


def all_to_all(x, axes):
    return lax.all_to_all(x, axes, split_axis=0, concat_axis=0, tiled=True)


def body(features, norm_gain, bias_hidden, gate_logit, w_in, w_out):
    rows = features.shape[0]
    high_count = lax.axis_size("seqhi")
    low_count = lax.axis_size("seqlo")
    high_bits = high_count.bit_length() - 1
    low_bits = low_count.bit_length() - 1
    layer_total = norm_gain.shape[0]

    def parts(w):
        high = lax.reduce_precision(w, exponent_bits=8, mantissa_bits=7)
        return high.astype(jnp.bfloat16), (w - high).astype(jnp.bfloat16)

    params = (norm_gain, bias_hidden, gate_logit, *parts(w_in), *parts(w_out))
    if rows % (8 * high_count * low_count) == 0:
        block = rows // (high_count * low_count)
        distances = [block * low_count * 2 ** (k % high_bits) for k in range(HI_LAYERS)]
        distances += [block * 2 ** (j % low_bits) for j in range(layer_total - HI_LAYERS)]
        states = all_to_all(features, ("seqhi", "seqlo"))
        states = run_layers(states, 0, distances, params, "all_layers")
        return all_to_all(states, ("seqhi", "seqlo"))
    high_distances = [rows // high_count * 2 ** (k % high_bits) for k in range(HI_LAYERS)]
    low_distances = [rows // low_count * 2 ** (j % low_bits) for j in range(layer_total - HI_LAYERS)]
    states = all_to_all(features, "seqhi")
    states = run_layers(states, 0, high_distances, params, "high_layers")
    states = all_to_all(states, "seqhi")
    states = all_to_all(states, "seqlo")
    states = run_layers(states, HI_LAYERS, low_distances, params, "low_layers")
    return all_to_all(states, "seqlo")


def solution(mesh):
    placed = (P(("seqhi", "seqlo"), None), P(), P(), P(), P(), P())
    return jax.shard_map(
        body, mesh=mesh, in_specs=placed, out_specs=P(("seqhi", "seqlo"), None), check_vma=False
    )
```

```python
import functools

import jax
import jax.numpy as jnp
from jax import lax
from jax.experimental import pallas as pl
from jax.experimental.pallas import tpu as pltpu
from jax.sharding import PartitionSpec as P

HI_LAYERS = 4
NORM_EPS = 1e-05
GELU_SCALE = 0.7978845608028654
GELU_CUBE = 0.044715


def split_high_low(x):
    high = x.astype(jnp.bfloat16)
    return high, (x - high.astype(jnp.float32)).astype(jnp.bfloat16)


def dot(a, b):
    return jnp.dot(a, b, preferred_element_type=jnp.float32)


def gelu(x):
    half = 0.5 * x
    return half + half * jnp.tanh(x * (GELU_SCALE + (GELU_SCALE * GELU_CUBE) * (x * x)))


def to_pairs(states, distance):
    rows, width = states.shape
    grouped = states.reshape(rows // (2 * distance), 2, distance, width)
    sides = [grouped[:, side].reshape(rows // 2, width) for side in range(2)]
    return jnp.concatenate(sides, axis=-1)


def from_pairs(pair, distance):
    half, double = pair.shape
    width = double // 2
    shape = (half // distance, 1, distance, width)
    sides = [pair[:, :width].reshape(shape), pair[:, width:].reshape(shape)]
    return jnp.concatenate(sides, axis=1).reshape(2 * half, width)


def scaled_center(pair, gain):
    center = pair - jnp.mean(pair, axis=-1, keepdims=True)
    return center, center * gain


def layers_kernel(
    first, distances, hidden_block,
    x_ref, gain_ref, bias_ref, gate_ref, in_high_ref, in_low_ref, out_high_any, out_low_any,
    y_ref, out_high_ref, out_low_ref, copied,
):
    pending = []
    for number, (source, target) in enumerate(
        [(out_high_any, out_high_ref), (out_low_any, out_low_ref)]
    ):
        copy = pltpu.make_async_copy(source, target, copied.at[number])
        copy.start()
        pending.append((target, copy))

    def load(ref):
        for target, copy in list(pending):
            if target is ref:
                copy.wait()
                pending.remove((target, copy))
        return ref[...]

    half = x_ref.shape[0] // 2
    hidden_count = in_high_ref.shape[1]
    blocks = [slice(c, c + hidden_block) for c in range(0, hidden_count, hidden_block)]
    layers = [(first + step, distance) for step, distance in enumerate(distances)]
    states, late = x_ref[...], None
    pair = to_pairs(states, distances[0])
    x_high = scaled_center(pair, gain_ref[first : first + 1, :])[1].astype(jnp.bfloat16)
    for step, (k, distance) in enumerate(layers):
        bias = bias_ref[k : k + 1, :]
        product_low = dot(x_high, in_low_ref[...])
        if late is not None:
            pair = to_pairs(from_pairs(near + late, distances[step - 1]), distance)
        center, scaled = scaled_center(pair, gain_ref[k : k + 1, :])
        scale = lax.rsqrt(jnp.mean(center * center, axis=-1, keepdims=True) + NORM_EPS)
        x_low = (scaled - x_high.astype(jnp.float32)).astype(jnp.bfloat16)
        stacked = jnp.concatenate([x_high, x_low], axis=0)
        parts = []
        for cols in blocks:
            both = dot(stacked, in_high_ref[:, cols])
            product = (both[:half] + both[half:]) + product_low[:, cols]
            parts.append(split_high_low(gelu(product * scale + bias[:, cols])))
        high = jnp.concatenate([part[0] for part in parts], axis=1)
        low = jnp.concatenate([part[1] for part in parts], axis=1)
        both = dot(jnp.concatenate([high, low], axis=0), load(out_high_ref))
        gate = jax.nn.sigmoid(gate_ref[k : k + 1, :])
        near = (gate * pair + both[:half]) + both[half:]
        late = dot(high, load(out_low_ref))
        if step + 1 < len(layers):
            following, next_distance = layers[step + 1]
            near_pair = to_pairs(from_pairs(near, distance), next_distance)
            scaled = scaled_center(near_pair, gain_ref[following : following + 1, :])[1]
            x_high = scaled.astype(jnp.bfloat16)
    y_ref[...] = from_pairs(near + late, distances[-1])


def run_layers(states, first, distances, params, name):
    rows, width = states.shape
    hidden = params[1].shape[1]
    kernel = functools.partial(layers_kernel, first, distances, min(hidden, 512))
    vmem = pl.BlockSpec(memory_space=pltpu.VMEM)
    return pl.pallas_call(
        kernel,
        out_shape=jax.ShapeDtypeStruct((rows, width), jnp.float32),
        in_specs=[vmem] * 6 + [pl.BlockSpec(memory_space=pl.ANY)] * 2,
        out_specs=vmem,
        scratch_shapes=[
            pltpu.VMEM(params[-2].shape, params[-2].dtype),
            pltpu.VMEM(params[-1].shape, params[-1].dtype),
            pltpu.SemaphoreType.DMA((2,)),
        ],
        compiler_params=pltpu.CompilerParams(vmem_limit_bytes=51 * 2**20),
        name=name,
    )(states, *params)


def all_to_all(x, axes):
    return lax.all_to_all(x, axes, split_axis=0, concat_axis=0, tiled=True)


def body(features, norm_gain, bias_hidden, gate_logit, w_in, w_out):
    rows = features.shape[0]
    high_count = lax.axis_size("seqhi")
    low_count = lax.axis_size("seqlo")
    high_bits = high_count.bit_length() - 1
    low_bits = low_count.bit_length() - 1
    layer_total = norm_gain.shape[0]

    def parts(w):
        high = lax.reduce_precision(w, exponent_bits=8, mantissa_bits=7)
        return high.astype(jnp.bfloat16), (w - high).astype(jnp.bfloat16)

    params = (norm_gain, bias_hidden, gate_logit, *parts(w_in), *parts(w_out))
    if rows % (8 * high_count * low_count) == 0:
        block = rows // (high_count * low_count)
        distances = [block * low_count * 2 ** (k % high_bits) for k in range(HI_LAYERS)]
        distances += [block * 2 ** (j % low_bits) for j in range(layer_total - HI_LAYERS)]
        states = all_to_all(features, ("seqhi", "seqlo"))
        states = run_layers(states, 0, distances, params, "all_layers")
        return all_to_all(states, ("seqhi", "seqlo"))
    high_distances = [rows // high_count * 2 ** (k % high_bits) for k in range(HI_LAYERS)]
    low_distances = [rows // low_count * 2 ** (j % low_bits) for j in range(layer_total - HI_LAYERS)]
    states = all_to_all(features, "seqhi")
    states = run_layers(states, 0, high_distances, params, "high_layers")
    states = all_to_all(states, "seqhi")
    states = all_to_all(states, "seqlo")
    states = run_layers(states, HI_LAYERS, low_distances, params, "low_layers")
    return all_to_all(states, "seqlo")


def solution(mesh):
    placed = (P(("seqhi", "seqlo"), None), P(), P(), P(), P(), P())
    return jax.shard_map(
        body, mesh=mesh, in_specs=placed, out_specs=P(("seqhi", "seqlo"), None), check_vma=False
    )
```

```python
import functools

import jax
import jax.numpy as jnp
from jax import lax
from jax.experimental import pallas as pl
from jax.experimental.pallas import tpu as pltpu
from jax.sharding import PartitionSpec as P

HI_LAYERS = 4
NORM_EPS = 1e-05
GELU_SCALE = 0.7978845608028654
GELU_CUBE = 0.044715


def split_high_low(x):
    high = x.astype(jnp.bfloat16)
    return high, (x - high.astype(jnp.float32)).astype(jnp.bfloat16)


def dot(a, b):
    return jnp.dot(a, b, preferred_element_type=jnp.float32)


def gelu(x):
    half = 0.5 * x
    return half + half * jnp.tanh(x * (GELU_SCALE + (GELU_SCALE * GELU_CUBE) * (x * x)))


def to_pairs(states, distance):
    rows, width = states.shape
    grouped = states.reshape(rows // (2 * distance), 2, distance, width)
    sides = [grouped[:, side].reshape(rows // 2, width) for side in range(2)]
    return jnp.concatenate(sides, axis=-1)


def from_pairs(pair, distance):
    half, double = pair.shape
    width = double // 2
    shape = (half // distance, 1, distance, width)
    sides = [pair[:, :width].reshape(shape), pair[:, width:].reshape(shape)]
    return jnp.concatenate(sides, axis=1).reshape(2 * half, width)


def scaled_center(pair, gain):
    center = pair - jnp.mean(pair, axis=-1, keepdims=True)
    return center, center * gain


def layers_kernel(
    first, distances, hidden_block,
    x_ref, gain_ref, bias_ref, gate_ref, in_high_ref, in_low_ref, out_high_any, out_low_any,
    y_ref, out_high_ref, out_low_ref, copied,
):
    pending = []
    for number, (source, target) in enumerate(
        [(out_high_any, out_high_ref), (out_low_any, out_low_ref)]
    ):
        copy = pltpu.make_async_copy(source, target, copied.at[number])
        copy.start()
        pending.append((target, copy))

    def load(ref):
        for target, copy in list(pending):
            if target is ref:
                copy.wait()
                pending.remove((target, copy))
        return ref[...]

    half = x_ref.shape[0] // 2
    hidden_count = in_high_ref.shape[1]
    blocks = [slice(c, c + hidden_block) for c in range(0, hidden_count, hidden_block)]
    layers = [(first + step, distance) for step, distance in enumerate(distances)]
    states, late = x_ref[...], None
    pair = to_pairs(states, distances[0])
    x_high = scaled_center(pair, gain_ref[first : first + 1, :])[1].astype(jnp.bfloat16)
    for step, (k, distance) in enumerate(layers):
        bias = bias_ref[k : k + 1, :]
        product_low = dot(x_high, in_low_ref[...])
        if late is not None:
            pair = to_pairs(from_pairs(near + late, distances[step - 1]), distance)
        center, scaled = scaled_center(pair, gain_ref[k : k + 1, :])
        scale = lax.rsqrt(jnp.mean(center * center, axis=-1, keepdims=True) + NORM_EPS)
        x_low = (scaled - x_high.astype(jnp.float32)).astype(jnp.bfloat16)
        stacked = jnp.concatenate([x_high, x_low], axis=0)
        parts = []
        for cols in blocks:
            both = dot(stacked, in_high_ref[:, cols])
            product = (both[:half] + both[half:]) + product_low[:, cols]
            parts.append(split_high_low(gelu(product * scale + bias[:, cols])))
        high = jnp.concatenate([part[0] for part in parts], axis=1)
        low = jnp.concatenate([part[1] for part in parts], axis=1)
        both = dot(jnp.concatenate([high, low], axis=0), load(out_high_ref))
        gate = jax.nn.sigmoid(gate_ref[k : k + 1, :])
        near = (gate * pair + both[:half]) + both[half:]
        late = dot(high, load(out_low_ref))
        if step + 1 < len(layers):
            following, next_distance = layers[step + 1]
            near_pair = to_pairs(from_pairs(near, distance), next_distance)
            scaled = scaled_center(near_pair, gain_ref[following : following + 1, :])[1]
            x_high = scaled.astype(jnp.bfloat16)
    y_ref[...] = from_pairs(near + late, distances[-1])


def run_layers(states, first, distances, params, name):
    rows, width = states.shape
    hidden = params[1].shape[1]
    kernel = functools.partial(layers_kernel, first, distances, min(hidden, 256))
    vmem = pl.BlockSpec(memory_space=pltpu.VMEM)
    return pl.pallas_call(
        kernel,
        out_shape=jax.ShapeDtypeStruct((rows, width), jnp.float32),
        in_specs=[vmem] * 6 + [pl.BlockSpec(memory_space=pl.ANY)] * 2,
        out_specs=vmem,
        scratch_shapes=[
            pltpu.VMEM(params[-2].shape, params[-2].dtype),
            pltpu.VMEM(params[-1].shape, params[-1].dtype),
            pltpu.SemaphoreType.DMA((2,)),
        ],
        compiler_params=pltpu.CompilerParams(vmem_limit_bytes=51 * 2**20),
        name=name,
    )(states, *params)


def all_to_all(x, axes):
    return lax.all_to_all(x, axes, split_axis=0, concat_axis=0, tiled=True)


def body(features, norm_gain, bias_hidden, gate_logit, w_in, w_out):
    rows = features.shape[0]
    high_count = lax.axis_size("seqhi")
    low_count = lax.axis_size("seqlo")
    high_bits = high_count.bit_length() - 1
    low_bits = low_count.bit_length() - 1
    layer_total = norm_gain.shape[0]

    def parts(w):
        high = lax.reduce_precision(w, exponent_bits=8, mantissa_bits=7)
        return high.astype(jnp.bfloat16), (w - high).astype(jnp.bfloat16)

    params = (norm_gain, bias_hidden, gate_logit, *parts(w_in), *parts(w_out))
    if rows % (8 * high_count * low_count) == 0:
        block = rows // (high_count * low_count)
        distances = [block * low_count * 2 ** (k % high_bits) for k in range(HI_LAYERS)]
        distances += [block * 2 ** (j % low_bits) for j in range(layer_total - HI_LAYERS)]
        states = all_to_all(features, ("seqhi", "seqlo"))
        states = run_layers(states, 0, distances, params, "all_layers")
        return all_to_all(states, ("seqhi", "seqlo"))
    high_distances = [rows // high_count * 2 ** (k % high_bits) for k in range(HI_LAYERS)]
    low_distances = [rows // low_count * 2 ** (j % low_bits) for j in range(layer_total - HI_LAYERS)]
    states = all_to_all(features, "seqhi")
    states = run_layers(states, 0, high_distances, params, "high_layers")
    states = all_to_all(states, "seqhi")
    states = all_to_all(states, "seqlo")
    states = run_layers(states, HI_LAYERS, low_distances, params, "low_layers")
    return all_to_all(states, "seqlo")


def solution(mesh):
    placed = (P(("seqhi", "seqlo"), None), P(), P(), P(), P(), P())
    return jax.shard_map(
        body, mesh=mesh, in_specs=placed, out_specs=P(("seqhi", "seqlo"), None), check_vma=False
    )
```

```python
import functools

import jax
import jax.numpy as jnp
from jax import lax
from jax.experimental import pallas as pl
from jax.experimental.pallas import tpu as pltpu
from jax.sharding import PartitionSpec as P

HI_LAYERS = 4
NORM_EPS = 1e-05
GELU_SCALE = 0.7978845608028654
GELU_CUBE = 0.044715


def split_high_low(x):
    high = x.astype(jnp.bfloat16)
    return high, (x - high.astype(jnp.float32)).astype(jnp.bfloat16)


def dot(a, b):
    return jnp.dot(a, b, preferred_element_type=jnp.float32)


def gelu(x):
    half = 0.5 * x
    return half + half * jnp.tanh(x * (GELU_SCALE + (GELU_SCALE * GELU_CUBE) * (x * x)))


def to_pairs(states, distance):
    rows, width = states.shape
    grouped = states.reshape(rows // (2 * distance), 2, distance, width)
    sides = [grouped[:, side].reshape(rows // 2, width) for side in range(2)]
    return jnp.concatenate(sides, axis=-1)


def from_pairs(pair, distance):
    half, double = pair.shape
    width = double // 2
    shape = (half // distance, 1, distance, width)
    sides = [pair[:, :width].reshape(shape), pair[:, width:].reshape(shape)]
    return jnp.concatenate(sides, axis=1).reshape(2 * half, width)


def scaled_center(pair, gain):
    center = pair - jnp.mean(pair, axis=-1, keepdims=True)
    return center, center * gain


def layers_kernel(
    first, distances, hidden_block,
    x_ref, gain_ref, bias_ref, gate_ref, in_high_ref, in_low_ref, out_high_any, out_low_any,
    y_ref, out_high_ref, out_low_ref, copied,
):
    pending = []
    for number, (source, target) in enumerate(
        [(out_high_any, out_high_ref), (out_low_any, out_low_ref)]
    ):
        copy = pltpu.make_async_copy(source, target, copied.at[number])
        copy.start()
        pending.append((target, copy))

    def load(ref):
        for target, copy in list(pending):
            if target is ref:
                copy.wait()
                pending.remove((target, copy))
        return ref[...]

    half = x_ref.shape[0] // 2
    hidden_count = in_high_ref.shape[1]
    blocks = [slice(c, c + hidden_block) for c in range(0, hidden_count, hidden_block)]
    layers = [(first + step, distance) for step, distance in enumerate(distances)]
    states, late = x_ref[...], None
    pair = to_pairs(states, distances[0])
    x_high = scaled_center(pair, gain_ref[first : first + 1, :])[1].astype(jnp.bfloat16)
    for step, (k, distance) in enumerate(layers):
        bias = bias_ref[k : k + 1, :]
        ahead = max(1, len(blocks) // 2)
        low_products = [dot(x_high, in_low_ref[:, cols]) for cols in blocks[:ahead]]
        if late is not None:
            pair = to_pairs(from_pairs(near + late, distances[step - 1]), distance)
        center, scaled = scaled_center(pair, gain_ref[k : k + 1, :])
        scale = lax.rsqrt(jnp.mean(center * center, axis=-1, keepdims=True) + NORM_EPS)
        x_low = (scaled - x_high.astype(jnp.float32)).astype(jnp.bfloat16)
        stacked = jnp.concatenate([x_high, x_low], axis=0)
        parts = []
        for number, cols in enumerate(blocks):
            both = dot(stacked, in_high_ref[:, cols])
            if ahead + number < len(blocks):
                low_products.append(dot(x_high, in_low_ref[:, blocks[ahead + number]]))
            product = (both[:half] + both[half:]) + low_products[number]
            parts.append(split_high_low(gelu(product * scale + bias[:, cols])))
        high = jnp.concatenate([part[0] for part in parts], axis=1)
        low = jnp.concatenate([part[1] for part in parts], axis=1)
        both = dot(jnp.concatenate([high, low], axis=0), load(out_high_ref))
        gate = jax.nn.sigmoid(gate_ref[k : k + 1, :])
        near = (gate * pair + both[:half]) + both[half:]
        late = dot(high, load(out_low_ref))
        if step + 1 < len(layers):
            following, next_distance = layers[step + 1]
            near_pair = to_pairs(from_pairs(near, distance), next_distance)
            scaled = scaled_center(near_pair, gain_ref[following : following + 1, :])[1]
            x_high = scaled.astype(jnp.bfloat16)
    y_ref[...] = from_pairs(near + late, distances[-1])


def run_layers(states, first, distances, params, name):
    rows, width = states.shape
    hidden = params[1].shape[1]
    kernel = functools.partial(layers_kernel, first, distances, min(hidden, 256))
    vmem = pl.BlockSpec(memory_space=pltpu.VMEM)
    return pl.pallas_call(
        kernel,
        out_shape=jax.ShapeDtypeStruct((rows, width), jnp.float32),
        in_specs=[vmem] * 6 + [pl.BlockSpec(memory_space=pl.ANY)] * 2,
        out_specs=vmem,
        scratch_shapes=[
            pltpu.VMEM(params[-2].shape, params[-2].dtype),
            pltpu.VMEM(params[-1].shape, params[-1].dtype),
            pltpu.SemaphoreType.DMA((2,)),
        ],
        compiler_params=pltpu.CompilerParams(vmem_limit_bytes=51 * 2**20),
        name=name,
    )(states, *params)


def all_to_all(x, axes):
    return lax.all_to_all(x, axes, split_axis=0, concat_axis=0, tiled=True)


def body(features, norm_gain, bias_hidden, gate_logit, w_in, w_out):
    rows = features.shape[0]
    high_count = lax.axis_size("seqhi")
    low_count = lax.axis_size("seqlo")
    high_bits = high_count.bit_length() - 1
    low_bits = low_count.bit_length() - 1
    layer_total = norm_gain.shape[0]

    def parts(w):
        high = lax.reduce_precision(w, exponent_bits=8, mantissa_bits=7)
        return high.astype(jnp.bfloat16), (w - high).astype(jnp.bfloat16)

    params = (norm_gain, bias_hidden, gate_logit, *parts(w_in), *parts(w_out))
    if rows % (8 * high_count * low_count) == 0:
        block = rows // (high_count * low_count)
        distances = [block * low_count * 2 ** (k % high_bits) for k in range(HI_LAYERS)]
        distances += [block * 2 ** (j % low_bits) for j in range(layer_total - HI_LAYERS)]
        states = all_to_all(features, ("seqhi", "seqlo"))
        states = run_layers(states, 0, distances, params, "all_layers")
        return all_to_all(states, ("seqhi", "seqlo"))
    high_distances = [rows // high_count * 2 ** (k % high_bits) for k in range(HI_LAYERS)]
    low_distances = [rows // low_count * 2 ** (j % low_bits) for j in range(layer_total - HI_LAYERS)]
    states = all_to_all(features, "seqhi")
    states = run_layers(states, 0, high_distances, params, "high_layers")
    states = all_to_all(states, "seqhi")
    states = all_to_all(states, "seqlo")
    states = run_layers(states, HI_LAYERS, low_distances, params, "low_layers")
    return all_to_all(states, "seqlo")


def solution(mesh):
    placed = (P(("seqhi", "seqlo"), None), P(), P(), P(), P(), P())
    return jax.shard_map(
        body, mesh=mesh, in_specs=placed, out_specs=P(("seqhi", "seqlo"), None), check_vma=False
    )
```

```python
import functools

import jax
import jax.numpy as jnp
from jax import lax
from jax.experimental import pallas as pl
from jax.experimental.pallas import tpu as pltpu
from jax.sharding import PartitionSpec as P

HI_LAYERS = 4
NORM_EPS = 1e-05
GELU_SCALE = 0.7978845608028654
GELU_CUBE = 0.044715


def split_high_low(x):
    high = x.astype(jnp.bfloat16)
    return high, (x - high.astype(jnp.float32)).astype(jnp.bfloat16)


def dot(a, b):
    return jnp.dot(a, b, preferred_element_type=jnp.float32)


def gelu(x):
    half = 0.5 * x
    return half + half * jnp.tanh(x * (GELU_SCALE + (GELU_SCALE * GELU_CUBE) * (x * x)))


def to_pairs(states, distance):
    rows, width = states.shape
    grouped = states.reshape(rows // (2 * distance), 2, distance, width)
    sides = [grouped[:, side].reshape(rows // 2, width) for side in range(2)]
    return jnp.concatenate(sides, axis=-1)


def from_pairs(pair, distance):
    half, double = pair.shape
    width = double // 2
    shape = (half // distance, 1, distance, width)
    sides = [pair[:, :width].reshape(shape), pair[:, width:].reshape(shape)]
    return jnp.concatenate(sides, axis=1).reshape(2 * half, width)


def scaled_center(pair, gain):
    center = pair - jnp.mean(pair, axis=-1, keepdims=True)
    return center, center * gain


def layers_kernel(
    first, distances, hidden_block,
    x_ref, gain_ref, bias_ref, gate_ref, in_high_ref, in_low_ref, out_high_any, out_low_any,
    y_ref, out_high_ref, out_low_ref, copied,
):
    pending = []
    for number, (source, target) in enumerate(
        [(out_high_any, out_high_ref), (out_low_any, out_low_ref)]
    ):
        copy = pltpu.make_async_copy(source, target, copied.at[number])
        copy.start()
        pending.append((target, copy))

    def load(ref):
        for target, copy in list(pending):
            if target is ref:
                copy.wait()
                pending.remove((target, copy))
        return ref[...]

    half = x_ref.shape[0] // 2
    hidden_count = in_high_ref.shape[1]
    blocks = [slice(c, c + hidden_block) for c in range(0, hidden_count, hidden_block)]
    layers = [(first + step, distance) for step, distance in enumerate(distances)]
    states, late = x_ref[...], None
    pair = to_pairs(states, distances[0])
    x_high = scaled_center(pair, gain_ref[first : first + 1, :])[1].astype(jnp.bfloat16)
    for step, (k, distance) in enumerate(layers):
        bias = bias_ref[k : k + 1, :]
        product_low = dot(x_high, in_low_ref[...])
        if late is not None:
            pair = to_pairs(from_pairs(near + late, distances[step - 1]), distance)
        center, scaled = scaled_center(pair, gain_ref[k : k + 1, :])
        scale = lax.rsqrt(jnp.mean(center * center, axis=-1, keepdims=True) + NORM_EPS)
        x_low = (scaled - x_high.astype(jnp.float32)).astype(jnp.bfloat16)
        stacked = jnp.concatenate([x_high, x_low], axis=0)
        parts = []
        for cols in blocks:
            both = dot(stacked, in_high_ref[:, cols])
            product = (both[:half] + both[half:]) + product_low[:, cols]
            parts.append(split_high_low(gelu(product * scale + bias[:, cols])))
        high = jnp.concatenate([part[0] for part in parts], axis=1)
        low = jnp.concatenate([part[1] for part in parts], axis=1)
        both = dot(jnp.concatenate([high, low], axis=0), load(out_high_ref))
        gate = jax.nn.sigmoid(gate_ref[k : k + 1, :])
        near = (gate * pair + both[:half]) + both[half:]
        late = dot(high, load(out_low_ref))
        if step + 1 < len(layers):
            following, next_distance = layers[step + 1]
            near_pair = to_pairs(from_pairs(near, distance), next_distance)
            scaled = scaled_center(near_pair, gain_ref[following : following + 1, :])[1]
            x_high = scaled.astype(jnp.bfloat16)
    y_ref[...] = from_pairs(near + late, distances[-1])


def run_layers(states, first, distances, params, name):
    rows, width = states.shape
    hidden = params[1].shape[1]
    kernel = functools.partial(layers_kernel, first, distances, hidden)
    vmem = pl.BlockSpec(memory_space=pltpu.VMEM)
    return pl.pallas_call(
        kernel,
        out_shape=jax.ShapeDtypeStruct((rows, width), jnp.float32),
        in_specs=[vmem] * 6 + [pl.BlockSpec(memory_space=pl.ANY)] * 2,
        out_specs=vmem,
        scratch_shapes=[
            pltpu.VMEM(params[-2].shape, params[-2].dtype),
            pltpu.VMEM(params[-1].shape, params[-1].dtype),
            pltpu.SemaphoreType.DMA((2,)),
        ],
        compiler_params=pltpu.CompilerParams(vmem_limit_bytes=51 * 2**20),
        name=name,
    )(states, *params)


def all_to_all(x, axes):
    return lax.all_to_all(x, axes, split_axis=0, concat_axis=0, tiled=True)


def body(features, norm_gain, bias_hidden, gate_logit, w_in, w_out):
    rows = features.shape[0]
    high_count = lax.axis_size("seqhi")
    low_count = lax.axis_size("seqlo")
    high_bits = high_count.bit_length() - 1
    low_bits = low_count.bit_length() - 1
    layer_total = norm_gain.shape[0]

    def parts(w):
        high = lax.reduce_precision(w, exponent_bits=8, mantissa_bits=7)
        return high.astype(jnp.bfloat16), (w - high).astype(jnp.bfloat16)

    params = (norm_gain, bias_hidden, gate_logit, *parts(w_in), *parts(w_out))
    if rows % (8 * high_count * low_count) == 0:
        block = rows // (high_count * low_count)
        distances = [block * low_count * 2 ** (k % high_bits) for k in range(HI_LAYERS)]
        distances += [block * 2 ** (j % low_bits) for j in range(layer_total - HI_LAYERS)]
        states = all_to_all(features, ("seqhi", "seqlo"))
        states = run_layers(states, 0, distances, params, "all_layers")
        return all_to_all(states, ("seqhi", "seqlo"))
    high_distances = [rows // high_count * 2 ** (k % high_bits) for k in range(HI_LAYERS)]
    low_distances = [rows // low_count * 2 ** (j % low_bits) for j in range(layer_total - HI_LAYERS)]
    states = all_to_all(features, "seqhi")
    states = run_layers(states, 0, high_distances, params, "high_layers")
    states = all_to_all(states, "seqhi")
    states = all_to_all(states, "seqlo")
    states = run_layers(states, HI_LAYERS, low_distances, params, "low_layers")
    return all_to_all(states, "seqlo")


def solution(mesh):
    placed = (P(("seqhi", "seqlo"), None), P(), P(), P(), P(), P())
    return jax.shard_map(
        body, mesh=mesh, in_specs=placed, out_specs=P(("seqhi", "seqlo"), None), check_vma=False
    )
```

```python
import functools

import jax
import jax.numpy as jnp
from jax import lax
from jax.experimental import pallas as pl
from jax.experimental.pallas import tpu as pltpu
from jax.sharding import PartitionSpec as P

HI_LAYERS = 4
NORM_EPS = 1e-05
GELU_SCALE = 0.7978845608028654
GELU_CUBE = 0.044715


def split_high_low(x):
    high = x.astype(jnp.bfloat16)
    return high, (x - high.astype(jnp.float32)).astype(jnp.bfloat16)


def dot(a, b):
    return jnp.dot(a, b, preferred_element_type=jnp.float32)


def gelu(x):
    half = 0.5 * x
    return half + half * jnp.tanh(x * (GELU_SCALE + (GELU_SCALE * GELU_CUBE) * (x * x)))


def to_pairs(states, distance):
    rows, width = states.shape
    grouped = states.reshape(rows // (2 * distance), 2, distance, width)
    sides = [grouped[:, side].reshape(rows // 2, width) for side in range(2)]
    return jnp.concatenate(sides, axis=-1)


def from_pairs(pair, distance):
    half, double = pair.shape
    width = double // 2
    shape = (half // distance, 1, distance, width)
    sides = [pair[:, :width].reshape(shape), pair[:, width:].reshape(shape)]
    return jnp.concatenate(sides, axis=1).reshape(2 * half, width)


def scaled_center(pair, gain):
    center = pair - jnp.mean(pair, axis=-1, keepdims=True)
    return center, center * gain


def layers_kernel(
    first, distances, hidden_block, factor,
    x_ref, gain_ref, bias_ref, gate_ref, in_high_ref, in_low_ref, out_high_any, out_low_any,
    y_ref, out_high_ref, out_low_ref, copied,
):
    pending = []
    for number, (source, target) in enumerate(
        [(out_high_any, out_high_ref), (out_low_any, out_low_ref)]
    ):
        copy = pltpu.make_async_copy(source, target, copied.at[number])
        copy.start()
        pending.append((target, copy))

    def load(ref):
        for target, copy in list(pending):
            if target is ref:
                copy.wait()
                pending.remove((target, copy))
        return ref[...]

    half = x_ref.shape[0] // 2
    hidden_count = in_high_ref.shape[1]
    blocks = [slice(c, c + hidden_block) for c in range(0, hidden_count, hidden_block)]
    layers = [(first + step, distance) for step, distance in enumerate(distances)]
    states, late = x_ref[...], None
    pair = to_pairs(states, distances[0])
    x_high = scaled_center(pair, gain_ref[first : first + 1, :])[1].astype(jnp.bfloat16)
    for step, (k, distance) in enumerate(layers):
        bias = bias_ref[k : k + 1, :]
        product_low = dot(x_high, in_low_ref[...])
        if late is not None:
            pair = to_pairs(from_pairs(near + late, distances[step - 1]), distance)
        center, scaled = scaled_center(pair, gain_ref[k : k + 1, :])
        scale = lax.rsqrt(jnp.mean(center * center, axis=-1, keepdims=True) + NORM_EPS)
        x_low = (scaled - x_high.astype(jnp.float32)).astype(jnp.bfloat16)
        stacked = jnp.concatenate([x_high, x_low], axis=0)
        parts = []
        for cols in blocks:
            both = dot(stacked, in_high_ref[:, cols])
            product = (both[:half] + both[half:]) + product_low[:, cols]
            parts.append(split_high_low(gelu(product * scale + bias[:, cols])))
        high = jnp.concatenate([part[0] for part in parts], axis=1)
        low = jnp.concatenate([part[1] for part in parts], axis=1)
        both = dot(jnp.concatenate([high, low], axis=0), load(out_high_ref))
        gate = jax.nn.sigmoid(gate_ref[k : k + 1, :])
        near = (gate * pair + both[:half]) + both[half:]
        late = dot(high, load(out_low_ref))
        if step + 1 < len(layers):
            following, next_distance = layers[step + 1]
            near_pair = to_pairs(from_pairs(near, distance), next_distance)
            scaled = scaled_center(near_pair, gain_ref[following : following + 1, :])[1]
            x_high = scaled.astype(jnp.bfloat16)
    y_ref[...] = factor * from_pairs(near + late, distances[-1])


def run_layers(states, first, distances, params, name, factor=1.0):
    rows, width = states.shape
    hidden = params[1].shape[1]
    kernel = functools.partial(layers_kernel, first, distances, min(hidden, 256), factor)
    vmem = pl.BlockSpec(memory_space=pltpu.VMEM)
    return pl.pallas_call(
        kernel,
        out_shape=jax.ShapeDtypeStruct((rows, width), jnp.float32),
        in_specs=[vmem] * 6 + [pl.BlockSpec(memory_space=pl.ANY)] * 2,
        out_specs=vmem,
        scratch_shapes=[
            pltpu.VMEM(params[-2].shape, params[-2].dtype),
            pltpu.VMEM(params[-1].shape, params[-1].dtype),
            pltpu.SemaphoreType.DMA((2,)),
        ],
        compiler_params=pltpu.CompilerParams(vmem_limit_bytes=51 * 2**20),
        name=name,
    )(states, *params)


def all_to_all(x, axes):
    return lax.all_to_all(x, axes, split_axis=0, concat_axis=0, tiled=True)


def body(features, norm_gain, bias_hidden, gate_logit, w_in, w_out):
    rows = features.shape[0]
    high_count = lax.axis_size("seqhi")
    low_count = lax.axis_size("seqlo")
    high_bits = high_count.bit_length() - 1
    low_bits = low_count.bit_length() - 1
    layer_total = norm_gain.shape[0]

    def parts(w):
        high = lax.reduce_precision(w, exponent_bits=8, mantissa_bits=7)
        return high.astype(jnp.bfloat16), (w - high).astype(jnp.bfloat16)

    params = (norm_gain, bias_hidden, gate_logit, *parts(w_in), *parts(w_out))
    if rows % (8 * high_count * low_count) == 0:
        block = rows // (high_count * low_count)
        distances = [block * low_count * 2 ** (k % high_bits) for k in range(HI_LAYERS)]
        distances += [block * 2 ** (j % low_bits) for j in range(layer_total - HI_LAYERS)]
        states = all_to_all(features, ("seqhi", "seqlo"))
        states = run_layers(states, 0, distances, params, "all_layers", 0.5)
        return 2.0 * all_to_all(states, ("seqhi", "seqlo"))
    high_distances = [rows // high_count * 2 ** (k % high_bits) for k in range(HI_LAYERS)]
    low_distances = [rows // low_count * 2 ** (j % low_bits) for j in range(layer_total - HI_LAYERS)]
    states = all_to_all(features, "seqhi")
    states = run_layers(states, 0, high_distances, params, "high_layers")
    states = all_to_all(states, "seqhi")
    states = all_to_all(states, "seqlo")
    states = run_layers(states, HI_LAYERS, low_distances, params, "low_layers")
    return all_to_all(states, "seqlo")


def solution(mesh):
    placed = (P(("seqhi", "seqlo"), None), P(), P(), P(), P(), P())
    return jax.shard_map(
        body, mesh=mesh, in_specs=placed, out_specs=P(("seqhi", "seqlo"), None), check_vma=False
    )
```

```python
import functools

import jax
import jax.numpy as jnp
from jax import lax
from jax.experimental import pallas as pl
from jax.experimental.pallas import tpu as pltpu
from jax.sharding import PartitionSpec as P

HI_LAYERS = 4
NORM_EPS = 1e-05
GELU_SCALE = 0.7978845608028654
GELU_CUBE = 0.044715


def split_high_low(x):
    high = x.astype(jnp.bfloat16)
    return high, (x - high.astype(jnp.float32)).astype(jnp.bfloat16)


def dot(a, b):
    return jnp.dot(a, b, preferred_element_type=jnp.float32)


def gelu(x):
    half = 0.5 * x
    return half + half * jnp.tanh(x * (GELU_SCALE + (GELU_SCALE * GELU_CUBE) * (x * x)))


def to_pairs(states, distance):
    rows, width = states.shape
    grouped = states.reshape(rows // (2 * distance), 2, distance, width)
    sides = [grouped[:, side].reshape(rows // 2, width) for side in range(2)]
    return jnp.concatenate(sides, axis=-1)


def from_pairs(pair, distance):
    half, double = pair.shape
    width = double // 2
    shape = (half // distance, 1, distance, width)
    sides = [pair[:, :width].reshape(shape), pair[:, width:].reshape(shape)]
    return jnp.concatenate(sides, axis=1).reshape(2 * half, width)


def scaled_center(pair, gain):
    center = pair - jnp.mean(pair, axis=-1, keepdims=True)
    return center, center * gain


def layers_kernel(
    first, distances, hidden_block,
    x_ref, gain_ref, bias_ref, gate_ref, in_high_ref, in_low_ref, out_high_any, out_low_any,
    y_ref, out_high_ref, out_low_ref, copied,
):
    pending = []
    for number, (source, target) in enumerate(
        [(out_high_any, out_high_ref), (out_low_any, out_low_ref)]
    ):
        copy = pltpu.make_async_copy(source, target, copied.at[number])
        copy.start()
        pending.append((target, copy))

    def load(ref):
        for target, copy in list(pending):
            if target is ref:
                copy.wait()
                pending.remove((target, copy))
        return ref[...]

    half = x_ref.shape[0] // 2
    hidden_count = in_high_ref.shape[1]
    blocks = [slice(c, c + hidden_block) for c in range(0, hidden_count, hidden_block)]
    layers = [(first + step, distance) for step, distance in enumerate(distances)]
    states, late = x_ref[...], None
    pair = to_pairs(states, distances[0])
    x_high = scaled_center(pair, gain_ref[first : first + 1, :])[1].astype(jnp.bfloat16)
    for step, (k, distance) in enumerate(layers):
        bias = bias_ref[k : k + 1, :]
        product_low = dot(x_high, in_low_ref[...])
        if late is not None:
            pair = to_pairs(from_pairs(near + late, distances[step - 1]), distance)
        center, scaled = scaled_center(pair, gain_ref[k : k + 1, :])
        scale = lax.rsqrt(jnp.mean(center * center, axis=-1, keepdims=True) + NORM_EPS)
        x_low = (scaled - x_high.astype(jnp.float32)).astype(jnp.bfloat16)
        stacked = jnp.concatenate([x_high, x_low], axis=0)
        parts = []
        for cols in blocks:
            both = dot(stacked, in_high_ref[:, cols])
            product = (both[:half] + both[half:]) + product_low[:, cols]
            parts.append(split_high_low(gelu(product * scale + bias[:, cols])))
        high = jnp.concatenate([part[0] for part in parts], axis=1)
        low = jnp.concatenate([part[1] for part in parts], axis=1)
        both = dot(jnp.concatenate([high, low], axis=0), load(out_high_ref))
        gate = jax.nn.sigmoid(gate_ref[k : k + 1, :])
        near = (gate * pair + both[:half]) + both[half:]
        late = dot(high, load(out_low_ref))
        if step + 1 < len(layers):
            following, next_distance = layers[step + 1]
            near_pair = to_pairs(from_pairs(near, distance), next_distance)
            scaled = scaled_center(near_pair, gain_ref[following : following + 1, :])[1]
            x_high = scaled.astype(jnp.bfloat16)
    y_ref[...] = from_pairs(near + late, distances[-1])


def run_layers(states, first, distances, params, name):
    rows, width = states.shape
    hidden = params[1].shape[1]
    kernel = functools.partial(layers_kernel, first, distances, min(hidden, 256))
    vmem = pl.BlockSpec(memory_space=pltpu.VMEM)
    return pl.pallas_call(
        kernel,
        out_shape=jax.ShapeDtypeStruct((rows, width), jnp.float32),
        in_specs=[vmem] * 6 + [pl.BlockSpec(memory_space=pl.ANY)] * 2,
        out_specs=vmem,
        scratch_shapes=[
            pltpu.VMEM(params[-2].shape, params[-2].dtype),
            pltpu.VMEM(params[-1].shape, params[-1].dtype),
            pltpu.SemaphoreType.DMA((2,)),
        ],
        compiler_params=pltpu.CompilerParams(vmem_limit_bytes=50 * 2**20),
        name=name,
    )(states, *params)


def all_to_all(x, axes):
    return lax.all_to_all(x, axes, split_axis=0, concat_axis=0, tiled=True)


def body(features, norm_gain, bias_hidden, gate_logit, w_in, w_out):
    rows = features.shape[0]
    high_count = lax.axis_size("seqhi")
    low_count = lax.axis_size("seqlo")
    high_bits = high_count.bit_length() - 1
    low_bits = low_count.bit_length() - 1
    layer_total = norm_gain.shape[0]

    def parts(w):
        high = lax.reduce_precision(w, exponent_bits=8, mantissa_bits=7)
        return high.astype(jnp.bfloat16), (w - high).astype(jnp.bfloat16)

    params = (norm_gain, bias_hidden, gate_logit, *parts(w_in), *parts(w_out))
    if rows % (8 * high_count * low_count) == 0:
        block = rows // (high_count * low_count)
        distances = [block * low_count * 2 ** (k % high_bits) for k in range(HI_LAYERS)]
        distances += [block * 2 ** (j % low_bits) for j in range(layer_total - HI_LAYERS)]
        states = all_to_all(features, ("seqhi", "seqlo"))
        states = run_layers(states, 0, distances, params, "all_layers")
        return all_to_all(states, ("seqhi", "seqlo"))
    high_distances = [rows // high_count * 2 ** (k % high_bits) for k in range(HI_LAYERS)]
    low_distances = [rows // low_count * 2 ** (j % low_bits) for j in range(layer_total - HI_LAYERS)]
    states = all_to_all(features, "seqhi")
    states = run_layers(states, 0, high_distances, params, "high_layers")
    states = all_to_all(states, "seqhi")
    states = all_to_all(states, "seqlo")
    states = run_layers(states, HI_LAYERS, low_distances, params, "low_layers")
    return all_to_all(states, "seqlo")


def solution(mesh):
    placed = (P(("seqhi", "seqlo"), None), P(), P(), P(), P(), P())
    return jax.shard_map(
        body, mesh=mesh, in_specs=placed, out_specs=P(("seqhi", "seqlo"), None), check_vma=False
    )
```

```python
import functools

import jax
import jax.numpy as jnp
from jax import lax
from jax.experimental import pallas as pl
from jax.experimental.pallas import tpu as pltpu
from jax.sharding import PartitionSpec as P

HI_LAYERS = 4
NORM_EPS = 1e-05
GELU_SCALE = 0.7978845608028654
GELU_CUBE = 0.044715


def split_high_low(x):
    high = x.astype(jnp.bfloat16)
    return high, (x - high.astype(jnp.float32)).astype(jnp.bfloat16)


def dot(a, b):
    return jnp.dot(a, b, preferred_element_type=jnp.float32)


def gelu(x):
    half = 0.5 * x
    return half + half * jnp.tanh(x * (GELU_SCALE + (GELU_SCALE * GELU_CUBE) * (x * x)))


def to_pairs(states, distance):
    rows, width = states.shape
    grouped = states.reshape(rows // (2 * distance), 2, distance, width)
    sides = [grouped[:, side].reshape(rows // 2, width) for side in range(2)]
    return jnp.concatenate(sides, axis=-1)


def from_pairs(pair, distance):
    half, double = pair.shape
    width = double // 2
    shape = (half // distance, 1, distance, width)
    sides = [pair[:, :width].reshape(shape), pair[:, width:].reshape(shape)]
    return jnp.concatenate(sides, axis=1).reshape(2 * half, width)


def scaled_center(pair, gain):
    center = pair - jnp.mean(pair, axis=-1, keepdims=True)
    return center, center * gain


def layers_kernel(
    first, distances, hidden_block,
    x_ref, gain_ref, bias_ref, gate_ref, in_high_ref, in_low_ref, out_high_ref, out_low_any,
    y_ref, out_low_ref, copied,
):
    pending = []
    for number, (source, target) in enumerate(
        [(out_low_any, out_low_ref)]
    ):
        copy = pltpu.make_async_copy(source, target, copied.at[number])
        copy.start()
        pending.append((target, copy))

    def load(ref):
        for target, copy in list(pending):
            if target is ref:
                copy.wait()
                pending.remove((target, copy))
        return ref[...]

    half = x_ref.shape[0] // 2
    hidden_count = in_high_ref.shape[1]
    blocks = [slice(c, c + hidden_block) for c in range(0, hidden_count, hidden_block)]
    layers = [(first + step, distance) for step, distance in enumerate(distances)]
    states, late = x_ref[...], None
    pair = to_pairs(states, distances[0])
    x_high = scaled_center(pair, gain_ref[first : first + 1, :])[1].astype(jnp.bfloat16)
    for step, (k, distance) in enumerate(layers):
        bias = bias_ref[k : k + 1, :]
        product_low = dot(x_high, in_low_ref[...])
        if late is not None:
            pair = to_pairs(from_pairs(near + late, distances[step - 1]), distance)
        center, scaled = scaled_center(pair, gain_ref[k : k + 1, :])
        scale = lax.rsqrt(jnp.mean(center * center, axis=-1, keepdims=True) + NORM_EPS)
        x_low = (scaled - x_high.astype(jnp.float32)).astype(jnp.bfloat16)
        stacked = jnp.concatenate([x_high, x_low], axis=0)
        parts = []
        for cols in blocks:
            both = dot(stacked, in_high_ref[:, cols])
            product = (both[:half] + both[half:]) + product_low[:, cols]
            parts.append(split_high_low(gelu(product * scale + bias[:, cols])))
        high = jnp.concatenate([part[0] for part in parts], axis=1)
        low = jnp.concatenate([part[1] for part in parts], axis=1)
        both = dot(jnp.concatenate([high, low], axis=0), load(out_high_ref))
        gate = jax.nn.sigmoid(gate_ref[k : k + 1, :])
        near = (gate * pair + both[:half]) + both[half:]
        late = dot(high, load(out_low_ref))
        if step + 1 < len(layers):
            following, next_distance = layers[step + 1]
            near_pair = to_pairs(from_pairs(near, distance), next_distance)
            scaled = scaled_center(near_pair, gain_ref[following : following + 1, :])[1]
            x_high = scaled.astype(jnp.bfloat16)
    y_ref[...] = from_pairs(near + late, distances[-1])


def run_layers(states, first, distances, params, name):
    rows, width = states.shape
    hidden = params[1].shape[1]
    kernel = functools.partial(layers_kernel, first, distances, min(hidden, 256))
    vmem = pl.BlockSpec(memory_space=pltpu.VMEM)
    return pl.pallas_call(
        kernel,
        out_shape=jax.ShapeDtypeStruct((rows, width), jnp.float32),
        in_specs=[vmem] * 7 + [pl.BlockSpec(memory_space=pl.ANY)],
        out_specs=vmem,
        scratch_shapes=[
            pltpu.VMEM(params[-1].shape, params[-1].dtype),
            pltpu.SemaphoreType.DMA((1,)),
        ],
        compiler_params=pltpu.CompilerParams(vmem_limit_bytes=50 * 2**20),
        name=name,
    )(states, *params)


def all_to_all(x, axes):
    return lax.all_to_all(x, axes, split_axis=0, concat_axis=0, tiled=True)


def body(features, norm_gain, bias_hidden, gate_logit, w_in, w_out):
    rows = features.shape[0]
    high_count = lax.axis_size("seqhi")
    low_count = lax.axis_size("seqlo")
    high_bits = high_count.bit_length() - 1
    low_bits = low_count.bit_length() - 1
    layer_total = norm_gain.shape[0]

    def parts(w):
        high = lax.reduce_precision(w, exponent_bits=8, mantissa_bits=7)
        return high.astype(jnp.bfloat16), (w - high).astype(jnp.bfloat16)

    params = (norm_gain, bias_hidden, gate_logit, *parts(w_in), *parts(w_out))
    if rows % (8 * high_count * low_count) == 0:
        block = rows // (high_count * low_count)
        distances = [block * low_count * 2 ** (k % high_bits) for k in range(HI_LAYERS)]
        distances += [block * 2 ** (j % low_bits) for j in range(layer_total - HI_LAYERS)]
        states = all_to_all(features, ("seqhi", "seqlo"))
        states = run_layers(states, 0, distances, params, "all_layers")
        return all_to_all(states, ("seqhi", "seqlo"))
    high_distances = [rows // high_count * 2 ** (k % high_bits) for k in range(HI_LAYERS)]
    low_distances = [rows // low_count * 2 ** (j % low_bits) for j in range(layer_total - HI_LAYERS)]
    states = all_to_all(features, "seqhi")
    states = run_layers(states, 0, high_distances, params, "high_layers")
    states = all_to_all(states, "seqhi")
    states = all_to_all(states, "seqlo")
    states = run_layers(states, HI_LAYERS, low_distances, params, "low_layers")
    return all_to_all(states, "seqlo")


def solution(mesh):
    placed = (P(("seqhi", "seqlo"), None), P(), P(), P(), P(), P())
    return jax.shard_map(
        body, mesh=mesh, in_specs=placed, out_specs=P(("seqhi", "seqlo"), None), check_vma=False
    )
```
